512 devices in a mesh: space: 128 (over z, y, core), feat: 4 (over x).
Axes of the slice: x: 4, y: 8, z: 8, core: 2. Of those that a mesh axis runs over, the one named last changes fastest.
Arguments:
- node: bfloat16 [32768, 512], P('space', 'feat'), may hold values from -6 to 6
- edge_feat: bfloat16 [65536, 512], P('space'), may hold values from -24 to 24
- agg_grad: bfloat16 [32768, 512], P('space', 'feat'), may hold values from -24 to 24
- w_send: bfloat16 [512, 512], P(None, 'feat'), may hold values from -0.25 to 0.25
- w_recv: bfloat16 [512, 512], P(None, 'feat'), may hold values from -0.25 to 0.25
- w_edge: bfloat16 [512, 512], P(None, 'feat'), may hold values from -0.25 to 0.25
- w_out: bfloat16 [512, 512], P(None, 'feat'), may hold values from -0.25 to 0.25
- receivers: int32 [65536], P('space'), may hold values from 0 to 255
- edge_slot: int32 [65536], P('space'), may hold values from 0 to 511, as said below
- send_rows: int32 [128, 512], P('space'), may hold values from 0 to 255, as said below
Outputs:
- node_grad: float32 [32768, 512], P('space', 'feat')
- edge_grad: float32 [65536, 512], P('space', 'feat')
- grad_send: float32 [512, 512], P('space', 'feat')
- grad_recv: float32 [512, 512], P('space', 'feat')
- grad_edge: float32 [512, 512], P('space', 'feat')
- grad_out: float32 [512, 512], P('space', 'feat')
The draws below stay inside these ranges and needn't reach their ends.
Inputs may be any that keep to these rules, and one draw needn't show every extreme that they name: `edge_slot`: slot s = p * 4 + k of an edge of region d names the sender node p * 256 + send_rows[p, d * 4 + k]. Within each block send_rows[p, d * 4 to (d + 1) * 4 - 1] the rows are distinct.
All inputs are finite; a program needn't handle non-finite values.
Results may differ from the reference program's by a relative error of at most 0.0029.
Values may be sent and summed in bfloat16 or wider, within the bound.
No kernel may reach another device: no remote copies, remote signals or barrier semaphores. Data moves between devices by JAX's collectives and lax.ppermute only.
A program may use at most 64 MiB of HBM per device.

```python
import jax
import jax.numpy as jnp
from jax import lax

L = 512
NODE_DEV = 256
EDGE_DEV = 512
SLOTS_DEV = 512
CAP = 4
NODES = 32768
EDGES = 65536
N_SPACE = 128


def draw_send_rows(key, part):
    key = jax.random.fold_in(key, 11)
    scores = jax.random.randint(key, (N_SPACE, N_SPACE, NODE_DEV), 0, 1 << 20)
    scores = scores * NODE_DEV + lax.broadcasted_iota(jnp.int32, (N_SPACE, N_SPACE, NODE_DEV), 2)
    ordering = jnp.argsort(scores, axis=-1)[:, :, :CAP]
    return ordering.reshape(N_SPACE, SLOTS_DEV).astype(jnp.int32)


def draw_edge_slot(key, part):
    key = jax.random.fold_in(key, 23)
    count_key, dest_key, source_key, pick_key = jax.random.split(key, 4)
    far_counts = jax.random.randint(count_key, (N_SPACE, N_SPACE), 1, 3)
    far_counts = jnp.minimum(far_counts, CAP)
    full_dest = jax.random.randint(dest_key, (), 0, N_SPACE)
    full_source = jax.random.randint(source_key, (), 0, N_SPACE)
    dest_index = lax.broadcasted_iota(jnp.int32, (N_SPACE, N_SPACE), 0)
    source_index = lax.broadcasted_iota(jnp.int32, (N_SPACE, N_SPACE), 1)
    offset = (source_index - dest_index) % N_SPACE
    distance = jnp.minimum(offset, N_SPACE - offset)
    near = (distance <= 2) | (dest_index == full_dest) | (source_index == full_source)
    counts = jnp.where(near, CAP, far_counts).astype(jnp.int32)
    inclusive = jnp.cumsum(counts, axis=1).astype(jnp.int32)
    totals = inclusive[:, N_SPACE - 1]
    picks = jax.random.randint(pick_key, (N_SPACE, EDGE_DEV), 0, 1 << 24) % totals[:, None]
    source = jnp.sum((inclusive[:, None, :] <= picks[:, :, None]).astype(jnp.int32), axis=2)
    starts = jnp.take_along_axis(inclusive - counts, source, axis=1)
    slots = source * CAP + (picks - starts)
    slots = slots.at[:, 0].set(0)
    last_slot = (N_SPACE - 1) * CAP + counts[:, N_SPACE - 1] - 1
    slots = slots.at[:, EDGE_DEV - 1].set(last_slot)
    return slots.reshape(EDGES).astype(jnp.int32)


def place_ends(result, own_key, smallest, largest):
    index_at = [jax.random.randint(jax.random.fold_in(own_key, axis), (), 0, length) for axis, length in enumerate(result.shape)]
    widest = result.shape.index(max(result.shape))
    next_to = index_at[:widest] + [(index_at[widest] + 1) % result.shape[widest]] + index_at[widest + 1:]
    return result.at[tuple(index_at)].set(smallest).at[tuple(next_to)].set(largest)


def raised(drawn, own_key, source, target, shards_of, factor):
    def block_of(dim):
        return (jnp.arange(drawn.shape[dim]) // (drawn.shape[dim] // shards_of)).reshape((-1,) + (1,) * (drawn.ndim - 1 - dim))

    one_side = jax.random.permutation(own_key, shards_of)[block_of(target)]
    far = (block_of(target) + shards_of // 2) % shards_of
    return jnp.where((block_of(source) == one_side) | (block_of(source) == far), factor * drawn, drawn)


def steps_of(rng, dims, pieces, low, high):
    loudness, own = 1.0, jax.random.fold_in(rng, 6)
    for axis_at, parts in pieces:
        draws = jnp.exp(jax.random.uniform(jax.random.fold_in(own, axis_at), (parts,), jnp.float32, low / len(pieces), high / len(pieces)))
        loudness = loudness * jnp.repeat(draws, dims[axis_at] // parts).reshape([-1 if axis == axis_at else 1 for axis in range(len(dims))])
    return loudness


def centred(stream_key, dims, width, reach, shards=(), kind=jnp.bfloat16):
    result = width * jax.random.normal(stream_key, dims, jnp.float32)
    if shards:
        result = result * steps_of(stream_key, dims, shards, -0.22, 0.18)
    return jnp.clip(result, -reach, reach).astype(kind)


def gaussian_with(rng, shape, deviation, reach, cuts, heavy, kind=jnp.bfloat16):
    array = deviation * jax.random.normal(rng, shape, jnp.float32)
    if cuts:
        array = array * steps_of(rng, shape, cuts, -0.22, 0.18)
    return jnp.clip(raised(array, jax.random.fold_in(rng, 3), *heavy), -reach, reach).astype(kind)


def setup_inputs(seed: int = 0) -> dict:
    seeds = jax.random.split(jax.random.key(seed), 11)
    node = centred(seeds[0], (NODES, L), 1.0, 6.0, ((0, 128), (1, 4)))
    edge_feat = gaussian_with(seeds[1], (EDGES, L), 1.0, 24.0, ((0, 128),), (0, 1, 128, 5.5))
    agg_grad = gaussian_with(seeds[2], (NODES, L), 1.0, 24.0, ((0, 128), (1, 4)), (0, 1, 128, 5.5))
    w_send = centred(seeds[3], (L, L), L ** -0.5, 0.25, ((1, 4),))
    w_recv = centred(seeds[4], (L, L), L ** -0.5, 0.25, ((1, 4),))
    w_edge = centred(seeds[5], (L, L), L ** -0.5, 0.25, ((1, 4),))
    w_out = centred(seeds[6], (L, L), L ** -0.5, 0.25, ((1, 4),))
    receivers = place_ends(jax.random.randint(seeds[7], (EDGES,), 0, NODE_DEV), jax.random.fold_in(seeds[7], 1), 0, NODE_DEV - 1).astype(jnp.int32)
    edge_slot = draw_edge_slot(jax.random.fold_in(seeds[10], 71), 0)
    send_rows = draw_send_rows(jax.random.fold_in(seeds[10], 71), 0)
    return {"node": node, "edge_feat": edge_feat, "agg_grad": agg_grad, "w_send": w_send, "w_recv": w_recv, "w_edge": w_edge, "w_out": w_out, "receivers": receivers, "edge_slot": edge_slot, "send_rows": send_rows}


def reference(node, edge_feat, agg_grad, w_send, w_recv, w_edge, w_out, receivers, edge_slot, send_rows):
    model_width = node.shape[1]
    edge_blocks = edge_feat.reshape(N_SPACE, EDGE_DEV, model_width)
    recv_blocks = receivers.reshape(N_SPACE, EDGE_DEV)
    slot_blocks = edge_slot.reshape(N_SPACE, EDGE_DEV)
    regions = jnp.arange(N_SPACE, dtype=jnp.int32)

    def per_region(carry, inputs):
        weight_grads, node_total = carry
        region, edge_rows, recv_local, slots = inputs
        source = slots // CAP
        within = slots % CAP
        sender = source * NODE_DEV + send_rows[source, region * CAP + within]
        receiver = region * NODE_DEV + recv_local
        sender_rows = node[sender]
        receiver_rows = node[receiver]
        message_grad = agg_grad[receiver]
        pre_act = (jnp.dot(sender_rows, w_send, preferred_element_type=jnp.float32)
                   + jnp.dot(receiver_rows, w_recv, preferred_element_type=jnp.float32)
                   + jnp.dot(edge_rows, w_edge, preferred_element_type=jnp.float32))
        gate_sig = jax.nn.sigmoid(pre_act)
        activation = (pre_act * gate_sig).astype(jnp.bfloat16)
        act_grad = jnp.dot(message_grad, w_out, preferred_element_type=jnp.float32)
        hidden_grad = (act_grad * gate_sig * (1.0 + pre_act * (1.0 - gate_sig))).astype(jnp.bfloat16)
        new_grads = (
            weight_grads[0] + jnp.dot(sender_rows.T, hidden_grad, preferred_element_type=jnp.float32),
            weight_grads[1] + jnp.dot(receiver_rows.T, hidden_grad, preferred_element_type=jnp.float32),
            weight_grads[2] + jnp.dot(edge_rows.T, hidden_grad, preferred_element_type=jnp.float32),
            weight_grads[3] + jnp.dot(message_grad.T, activation, preferred_element_type=jnp.float32),
        )
        edge_out = jnp.dot(hidden_grad, w_edge.T, preferred_element_type=jnp.float32)
        send_terms = jnp.dot(hidden_grad, w_send.T, preferred_element_type=jnp.float32)
        recv_terms = jnp.dot(hidden_grad, w_recv.T, preferred_element_type=jnp.float32)
        node_total = node_total.at[sender].add(send_terms).at[receiver].add(recv_terms)
        return (new_grads, node_total), edge_out

    zero_weight = jnp.zeros((model_width, model_width), jnp.float32)
    init = ((zero_weight, zero_weight, zero_weight, zero_weight), jnp.zeros((NODES, model_width), jnp.float32))
    (weight_grads, node_grad), edge_out = lax.scan(per_region, init, (regions, edge_blocks, recv_blocks, slot_blocks))
    edge_grad = edge_out.reshape(EDGES, model_width)
    return (node_grad, edge_grad, weight_grads[0], weight_grads[1], weight_grads[2], weight_grads[3])
```

```python
import jax
import jax.numpy as jnp
from jax import lax
from jax.experimental import pallas as pl
from jax.experimental.pallas import tpu as pltpu
from jax.sharding import PartitionSpec as P

F32 = jnp.float32
BF16 = jnp.bfloat16
LANES = 128


def mm(a, b):
    return jnp.dot(a, b, preferred_element_type=F32)


def mm_nt(a, b):
    return lax.dot_general(a, b, (((1,), (1,)), ((), ())), preferred_element_type=F32)


def mm_tn(a, b):
    return lax.dot_general(a, b, (((0,), (0,)), ((), ())), preferred_element_type=F32)


def hot(mask):
    return jnp.where(mask, 1.0, 0.0).astype(BF16)


def hot_by_column(row, rows):
    shape = (rows, row.shape[1])
    return hot(lax.broadcasted_iota(jnp.int32, shape, 0) == row)


def hot_by_row(row, columns):
    count = row.shape[1]
    column = jnp.broadcast_to(row, (LANES, count)).T
    lane = lax.broadcasted_iota(jnp.int32, (count, LANES), 1)
    parts = [hot(column == lane + start) for start in range(0, columns, LANES)]
    return jnp.concatenate(parts, axis=1)


def join(ref, start, size):
    return jnp.concatenate([ref[q, start : start + size, :] for q in range(ref.shape[0])], axis=1)


def split_high_low(x):
    high = x.astype(BF16)
    return high, (x - high.astype(F32)).astype(BF16)


def first_kernel(node, agg, w_send, w_recv, w_edge, rows, shared, picked):
    count, quarter = node.shape
    for q in range(shared.shape[0]):
        block = slice(q * quarter, (q + 1) * quarter)
        shared[q, 0:count, :] = node[...]
        shared[q, count : 2 * count, :] = agg[...]
        for i, weight in enumerate((w_send, w_recv, w_edge)):
            start = 2 * count + i * quarter
            shared[q, start : start + quarter, :] = weight[block, :]
    picked[...] = mm(hot_by_row(rows[...], count), node[...]).astype(BF16)


def receiver_kernel(
    shared, edge_feat, w_recv, w_edge, w_out, receivers, slots,
    receiver_rows, message_grad, pre_part, act_grad, slot_hot,
):
    count = shared.shape[1] - 3 * LANES
    count = count // 2
    receive = hot_by_row(receivers[...], count)
    receiver_rows[...] = mm(receive, join(shared, 0, count)).astype(BF16)
    message_grad[...] = mm(receive, join(shared, count, count)).astype(BF16)
    pre_part[...] = mm(receiver_rows[...], w_recv[...]) + mm(edge_feat[...], w_edge[...])
    act_grad[...] = mm(message_grad[...], w_out[...])
    slot_hot[...] = hot_by_row(slots[...], slot_hot.shape[1])


def hidden_kernel(
    slot_rows, slot_hot, w_send, pre_part, act_grad, sender_rows, hidden, activation
):
    sender_rows[...] = mm(slot_hot[...], join(slot_rows, 0, slot_rows.shape[1])).astype(BF16)
    pre_act = mm(sender_rows[...], w_send[...]) + pre_part[...]
    gate = jax.nn.sigmoid(pre_act)
    activation[...] = (pre_act * gate).astype(BF16)
    grad = (act_grad[...] * gate * (1.0 + pre_act * (1.0 - gate))).astype(BF16)
    for q in range(hidden.shape[0]):
        hidden[q] = grad


def weight_kernel(
    core, sender_rows, receiver_rows, edge_feat, message_grad, hidden, activation, kept, given
):
    grad = hidden[0]
    size = sender_rows.shape[1]
    mine = core[0] == 0
    for i, (low, high, high_right) in enumerate(
        (
            (sender_rows, edge_feat, grad),
            (receiver_rows, message_grad, activation[...]),
        )
    ):
        low_sum = mm_tn(low[...], grad)
        high_sum = mm_tn(high[...], high_right)
        kept[i * size : (i + 1) * size, :] = jnp.where(mine, low_sum, high_sum)
        given[i * size : (i + 1) * size, :] = jnp.where(mine, high_sum, low_sum)


def payload_kernel(hidden, shared, slots, kept, taken, payload):
    size = kept.shape[0] // 2
    quarter = kept.shape[1]
    weights = shared.shape[1] - 3 * LANES
    w_send = join(shared, weights, LANES)
    sums = mm(hot_by_column(slots[...], payload.shape[0]), join(hidden, 0, hidden.shape[1]))
    high, low = split_high_low(sums)
    terms = mm_nt(high, w_send) + mm_nt(low, w_send)
    high, low = split_high_low(terms)
    payload[:, 0:quarter] = (kept[0:size, :] + taken[0:size, :]).astype(BF16)
    payload[:, quarter : 2 * quarter] = (kept[size:, :] + taken[size:, :]).astype(BF16)
    payload[:, 2 * quarter : 3 * quarter] = high
    payload[:, 3 * quarter : 4 * quarter] = low


def edge_kernel(hidden, shared, receivers, edge_grad, recv_part):
    full = join(hidden, 0, hidden.shape[1])
    weights = shared.shape[1] - 3 * LANES
    edge_grad[...] = mm_nt(full, join(shared, weights + 2 * LANES, LANES))
    sums = mm(hot_by_column(receivers[...], recv_part.shape[0]), full)
    high, low = split_high_low(sums)
    w_recv = join(shared, weights + LANES, LANES)
    recv_part[...] = mm_nt(high, w_recv) + mm_nt(low, w_recv)


def last_kernel(arrived, rows, recv_part, node_grad, grad_send, grad_recv, grad_edge, grad_out):
    quarter = node_grad.shape[1]
    slots = arrived.shape[0]
    back = mm(hot_by_column(rows[...], node_grad.shape[0]), arrived[:, 2 * quarter : 4 * quarter])
    node_grad[...] = recv_part[...] + (back[:, 0:quarter] + back[:, quarter:])
    shape = (8, slots)
    place = lax.broadcasted_iota(jnp.int32, shape, 1) % 8
    pick = hot(place == lax.broadcasted_iota(jnp.int32, shape, 0))
    sums = mm(pick, arrived[:, 0 : 2 * quarter])
    grad_send[...] = sums[0:4, 0:quarter]
    grad_recv[...] = sums[0:4, quarter:]
    grad_edge[...] = sums[4:8, 0:quarter]
    grad_out[...] = sums[4:8, quarter:]


def call(kernel, outs, *operands, scalars=0, flops=0):
    vmem = pl.BlockSpec(memory_space=pltpu.VMEM)
    smem = pl.BlockSpec(memory_space=pltpu.SMEM)
    moved = sum(x.size * x.dtype.itemsize for x in operands)
    moved += sum(x.size * x.dtype.itemsize for x in outs)
    return pl.pallas_call(
        kernel,
        out_shape=list(outs),
        in_specs=[smem] * scalars + [vmem] * (len(operands) - scalars),
        out_specs=[vmem] * len(outs),
        compiler_params=pltpu.CompilerParams(vmem_limit_bytes=24 * 1024 * 1024),
        cost_estimate=pl.CostEstimate(flops=flops, bytes_accessed=moved, transcendentals=0),
    )(*operands)


def local(
    node, edge_feat, agg_grad, w_send, w_recv, w_edge, w_out, receivers, edge_slot, send_rows
):
    spaces = lax.axis_size("space")
    feats = lax.axis_size("feat")
    slot_count = send_rows.shape[1]
    capacity = slot_count // spaces
    node_count, quarter = node.shape
    edges, width = edge_feat.shape
    sds = jax.ShapeDtypeStruct
    receivers = receivers.reshape(1, edges)
    slots = edge_slot.reshape(1, edges)
    core = (lax.axis_index("space") % 2).reshape(1)

    def over_feat(x):
        return lax.all_to_all(x, "feat", split_axis=0, concat_axis=0, tiled=True)

    def over_space(x):
        lanes = x.shape[1]
        moved = lax.all_to_all(
            x.reshape(spaces, capacity, lanes), "space", split_axis=0, concat_axis=0, tiled=True
        )
        return moved.reshape(slot_count, lanes)

    shared, picked = call(
        first_kernel,
        (
            sds((feats, 2 * node_count + 3 * quarter, quarter), BF16),
            sds((slot_count, quarter), BF16),
        ),
        node, agg_grad, w_send, w_recv, w_edge, send_rows,
        flops=2 * slot_count * node_count * quarter,
    )
    shared = over_feat(shared)
    arrived = over_space(picked)
    receiver_rows, message_grad, pre_part, act_grad, slot_hot = call(
        receiver_kernel,
        (
            sds((edges, width), BF16),
            sds((edges, width), BF16),
            sds((edges, quarter), F32),
            sds((edges, quarter), F32),
            sds((edges, slot_count), BF16),
        ),
        shared, edge_feat, w_recv, w_edge, w_out, receivers, slots,
        flops=4 * edges * width * (node_count + 2 * quarter),
    )
    slot_rows = over_feat(jnp.broadcast_to(arrived[None], (feats, slot_count, quarter)))
    sender_rows, hidden, activation = call(
        hidden_kernel,
        (
            sds((edges, width), BF16),
            sds((feats, edges, quarter), BF16),
            sds((edges, quarter), BF16),
        ),
        slot_rows, slot_hot, w_send, pre_part, act_grad,
        flops=2 * edges * width * (slot_count + quarter),
    )
    hidden_full = over_feat(hidden)
    kept, given = call(
        weight_kernel,
        (sds((2 * width, quarter), F32), sds((2 * width, quarter), F32)),
        core, sender_rows, receiver_rows, edge_feat, message_grad, hidden, activation,
        scalars=1,
        flops=8 * edges * width * quarter,
    )
    taken = lax.ppermute(given, "space", [(i, i ^ 1) for i in range(spaces)])
    (payload,) = call(
        payload_kernel,
        (sds((slot_count, 4 * quarter), BF16),),
        hidden_full, shared, slots, kept, taken,
        flops=2 * slot_count * width * (edges + 2 * quarter),
    )
    returned = over_space(payload)
    edge_grad, recv_part = call(
        edge_kernel,
        (sds((edges, quarter), F32), sds((node_count, quarter), F32)),
        hidden_full, shared, receivers,
        flops=2 * edges * width * (node_count + 2 * quarter),
    )
    small = sds((width // spaces, quarter), F32)
    node_grad, grad_send, grad_recv, grad_edge, grad_out = call(
        last_kernel,
        (sds((node_count, quarter), F32), small, small, small, small),
        returned, send_rows, recv_part,
        flops=4 * node_count * slot_count * quarter,
    )
    return (node_grad, edge_grad, grad_send, grad_recv, grad_edge, grad_out)


def solution(mesh):
    placed = (
        P("space", "feat"),
        P("space", None),
        P("space", "feat"),
        P(None, "feat"),
        P(None, "feat"),
        P(None, "feat"),
        P(None, "feat"),
        P("space"),
        P("space"),
        P("space", None),
    )
    return jax.shard_map(
        local,
        mesh=mesh,
        in_specs=placed,
        out_specs=(P("space", "feat"),) * 6,
        check_vma=False,
    )
```

```python
import jax
import jax.numpy as jnp
from jax import lax
from jax.experimental import pallas as pl
from jax.experimental.pallas import tpu as pltpu
from jax.sharding import PartitionSpec as P

F32 = jnp.float32
BF16 = jnp.bfloat16
LANES = 128


def mm(a, b):
    return jnp.dot(a, b, preferred_element_type=F32)


def mm_nt(a, b):
    return lax.dot_general(a, b, (((1,), (1,)), ((), ())), preferred_element_type=F32)


def mm_tn(a, b):
    return lax.dot_general(a, b, (((0,), (0,)), ((), ())), preferred_element_type=F32)


def hot(mask):
    return jnp.where(mask, 1.0, 0.0).astype(BF16)


def hot_by_column(row, rows):
    shape = (rows, row.shape[1])
    return hot(lax.broadcasted_iota(jnp.int32, shape, 0) == row)


def hot_by_row(row, columns):
    count = row.shape[1]
    column = jnp.broadcast_to(row, (LANES, count)).T
    lane = lax.broadcasted_iota(jnp.int32, (count, LANES), 1)
    parts = [hot(column == lane + start) for start in range(0, columns, LANES)]
    return jnp.concatenate(parts, axis=1)


def fetch(sems, *pairs):
    copies = [pltpu.make_async_copy(src, dst, sems.at[i]) for i, (src, dst) in enumerate(pairs)]
    for copy in copies:
        copy.start()
    return copies


def join(ref, start, size):
    return jnp.concatenate([ref[q, start : start + size, :] for q in range(ref.shape[0])], axis=1)


def split_high_low(x):
    high = x.astype(BF16)
    return high, (x - high.astype(F32)).astype(BF16)


def first_kernel(node, agg, rows, own, picked, rows_here, sems):
    count = node.shape[0]
    copies = fetch(
        sems,
        (rows, rows_here),
        (node, own.at[0:count, :]),
        (agg, own.at[count : 2 * count, :]),
    )
    copies[0].wait()
    pick = hot_by_row(rows_here[...], count)
    copies[1].wait()
    picked[...] = mm(pick, own[0:count, :]).astype(BF16)
    copies[2].wait()


def spread_kernel(rows, after, spread):
    del after
    for q in range(spread.shape[0]):
        spread[q] = rows[...]


def middle_kernel(
    core, shared, slot_rows, edge_feat, w_send, w_recv, w_edge, w_out, receivers, slots,
    kept, given, slot_sums, hidden,
):
    count = shared.shape[1] // 2
    size = edge_feat.shape[1]
    receive = hot_by_row(receivers[...], count)
    receiver_rows = mm(receive, join(shared, 0, count)).astype(BF16)
    message_grad = mm(receive, join(shared, count, count)).astype(BF16)
    act_grad = mm(message_grad, w_out[...])
    pre_act = mm(receiver_rows, w_recv[...]) + mm(edge_feat[...], w_edge[...])
    slot_hot = hot_by_row(slots[...], slot_rows.shape[1])
    sender_rows = mm(slot_hot, join(slot_rows, 0, slot_rows.shape[1])).astype(BF16)
    pre_act += mm(sender_rows, w_send[...])
    gate = jax.nn.sigmoid(pre_act)
    activation = (pre_act * gate).astype(BF16)
    grad = (act_grad * gate * (1.0 + pre_act * (1.0 - gate))).astype(BF16)
    hidden[...] = grad
    mine = core[0] == 0
    for i, (low, high, high_right) in enumerate(
        (
            (sender_rows, edge_feat[...], grad),
            (receiver_rows, message_grad, activation),
        )
    ):
        low_sum = mm_tn(low, grad)
        high_sum = mm_tn(high, high_right)
        kept[i * size : (i + 1) * size, :] = jnp.where(mine, low_sum, high_sum)
        given[i * size : (i + 1) * size, :] = jnp.where(mine, high_sum, low_sum)
    slot_sums[...] = mm(hot_by_column(slots[...], slot_sums.shape[0]), grad).astype(BF16)


def payload_kernel(kept, taken, sums, payload):
    size = kept.shape[0] // 2
    quarter = kept.shape[1]
    payload[:, 0:quarter] = (kept[0:size, :] + taken[0:size, :]).astype(BF16)
    payload[:, quarter : 2 * quarter] = (kept[size:, :] + taken[size:, :]).astype(BF16)
    payload[:, 2 * quarter : 3 * quarter] = sums[...]


def edge_kernel(place, hidden, w_edge, receivers, mine, *rest):
    *theirs, recv_sums = rest
    quarter = mine.shape[1]
    feats = 1 + len(theirs)
    for step, out in enumerate((mine, *theirs)):
        start = pl.multiple_of(lax.rem(place[0] + step, feats) * quarter, quarter)
        part = mm_nt(hidden[...], w_edge[pl.ds(start, quarter), :])
        out[...] = part.astype(out.dtype)
    recv_sums[...] = mm(hot_by_column(receivers[...], recv_sums.shape[0]), hidden[...])


def node_part_kernel(
    arrived, rows, recv_sums, w_send, w_recv, mine, *rest
):
    *theirs, parts, edge_grad, grad_send, grad_recv, grad_edge, grad_out = rest
    quarter = recv_sums.shape[1]
    back = mm(
        hot_by_column(rows[...], recv_sums.shape[0]), arrived[:, 2 * quarter : 3 * quarter]
    )
    total = 0.0
    for sums, weight in ((back, w_send), (recv_sums[...], w_recv)):
        high, low = split_high_low(sums)
        total += mm_nt(high, weight[...]) + mm_nt(low, weight[...])
    for q in range(parts.shape[0]):
        parts[q] = total[:, q * quarter : (q + 1) * quarter].astype(BF16)
    edge_total = mine[...]
    for part in theirs:
        edge_total += part[...].astype(F32)
    edge_grad[...] = edge_total
    shape = (8, arrived.shape[0])
    place = lax.broadcasted_iota(jnp.int32, shape, 1) % 8
    pick = hot(place == lax.broadcasted_iota(jnp.int32, shape, 0))
    sums = mm(pick, arrived[:, 0 : 2 * quarter])
    grad_send[...] = sums[0:4, 0:quarter]
    grad_recv[...] = sums[0:4, quarter:]
    grad_edge[...] = sums[4:8, 0:quarter]
    grad_out[...] = sums[4:8, quarter:]


def node_sum_kernel(parts, node_grad):
    total = parts[0].astype(F32)
    for q in range(1, parts.shape[0]):
        total += parts[q].astype(F32)
    node_grad[...] = total


ANY = pl.BlockSpec(memory_space=pl.ANY)
VMEM = pl.BlockSpec(memory_space=pltpu.VMEM)
SMEM = pl.BlockSpec(memory_space=pltpu.SMEM)


def call(kernel, outs, *operands, places=None, scratch=(), flops=0, limit=24 * 1024 * 1024):
    moved = sum(x.size * x.dtype.itemsize for x in operands)
    moved += sum(x.size * x.dtype.itemsize for x in outs)
    return pl.pallas_call(
        kernel,
        out_shape=list(outs),
        in_specs=list(places or [VMEM] * len(operands)),
        out_specs=[VMEM] * len(outs),
        scratch_shapes=list(scratch),
        compiler_params=pltpu.CompilerParams(vmem_limit_bytes=limit),
        cost_estimate=pl.CostEstimate(flops=flops, bytes_accessed=moved, transcendentals=0),
    )(*operands)


def local(
    node, edge_feat, agg_grad, w_send, w_recv, w_edge, w_out, receivers, edge_slot, send_rows
):
    spaces = lax.axis_size("space")
    feats = lax.axis_size("feat")
    slot_count = send_rows.shape[1]
    capacity = slot_count // spaces
    node_count, quarter = node.shape
    edges, width = edge_feat.shape
    sds = jax.ShapeDtypeStruct
    receivers = receivers.reshape(1, edges)
    slots = edge_slot.reshape(1, edges)
    core = (lax.axis_index("space") % 2).reshape(1)
    place = lax.axis_index("feat").reshape(1)

    def over_feat(x):
        return lax.all_to_all(x, "feat", split_axis=0, concat_axis=0, tiled=True)

    def over_space(x):
        lanes = x.shape[1]
        moved = lax.all_to_all(
            x.reshape(spaces, capacity, lanes), "space", split_axis=0, concat_axis=0, tiled=True
        )
        return moved.reshape(slot_count, lanes)

    own, picked = call(
        first_kernel,
        (sds((2 * node_count, quarter), BF16), sds((slot_count, quarter), BF16)),
        node, agg_grad, send_rows,
        places=[ANY] * 3,
        scratch=[pltpu.VMEM(send_rows.shape, jnp.int32), pltpu.SemaphoreType.DMA((3,))],
        flops=2 * slot_count * node_count * quarter,
        limit=60 * 1024 * 1024,
    )
    arrived = over_space(picked)
    shared = lax.all_gather(own, "feat", axis=0, tiled=False)
    (spread,) = call(
        spread_kernel,
        (sds((feats, slot_count, quarter), BF16),),
        arrived, shared,
        places=[VMEM, ANY],
    )
    slot_rows = over_feat(spread)
    kept, given, slot_sums, hidden = call(
        middle_kernel,
        (
            sds((2 * width, quarter), F32),
            sds((2 * width, quarter), F32),
            sds((slot_count, quarter), BF16),
            sds((edges, quarter), BF16),
        ),
        core, shared, slot_rows, edge_feat, w_send, w_recv, w_edge, w_out, receivers, slots,
        places=[SMEM] + [VMEM] * 9,
        flops=2 * edges * width * (2 * node_count + 2 * slot_count + 8 * quarter),
    )
    taken = lax.ppermute(given, "space", [(i, i ^ 1) for i in range(spaces)])
    (payload,) = call(
        payload_kernel, (sds((slot_count, 3 * quarter), BF16),), kept, taken, slot_sums
    )
    payload, hidden = lax.optimization_barrier((payload, hidden))
    returned = over_space(payload)
    part = sds((edges, quarter), BF16)
    mine, *theirs, recv_sums = call(
        edge_kernel,
        (sds((edges, quarter), F32), *[part] * (feats - 1), sds((node_count, quarter), F32)),
        place, hidden, w_edge, receivers,
        places=[SMEM] + [VMEM] * 3,
        flops=2 * edges * quarter * (width + node_count),
    )
    theirs = [
        lax.ppermute(x, "feat", [(i, (i + step) % feats) for i in range(feats)])
        for step, x in enumerate(theirs, 1)
    ]
    small = sds((width // spaces, quarter), F32)
    parts, edge_grad, grad_send, grad_recv, grad_edge, grad_out = call(
        node_part_kernel,
        (
            sds((feats, node_count, quarter), BF16),
            sds((edges, quarter), F32),
            small, small, small, small,
        ),
        returned, send_rows, recv_sums, w_send, w_recv, mine, *theirs,
        flops=2 * node_count * quarter * (slot_count + 4 * width),
    )
    (node_grad,) = call(
        node_sum_kernel, (sds((node_count, quarter), F32),), over_feat(parts)
    )
    return (node_grad, edge_grad, grad_send, grad_recv, grad_edge, grad_out)


def solution(mesh):
    placed = (
        P("space", "feat"),
        P("space", None),
        P("space", "feat"),
        P(None, "feat"),
        P(None, "feat"),
        P(None, "feat"),
        P(None, "feat"),
        P("space"),
        P("space"),
        P("space", None),
    )
    return jax.shard_map(
        local,
        mesh=mesh,
        in_specs=placed,
        out_specs=(P("space", "feat"),) * 6,
        check_vma=False,
    )
```

```python
import jax
import jax.numpy as jnp
from jax import lax
from jax.experimental import pallas as pl
from jax.experimental.pallas import tpu as pltpu
from jax.sharding import PartitionSpec as P

F32 = jnp.float32
BF16 = jnp.bfloat16
LANES = 128


def mm(a, b):
    return jnp.dot(a, b, preferred_element_type=F32)


def mm_nt(a, b):
    return lax.dot_general(a, b, (((1,), (1,)), ((), ())), preferred_element_type=F32)


def mm_tn(a, b):
    return lax.dot_general(a, b, (((0,), (0,)), ((), ())), preferred_element_type=F32)


def hot(mask):
    return jnp.where(mask, 1.0, 0.0).astype(BF16)


def hot_by_column(row, rows):
    shape = (rows, row.shape[1])
    return hot(lax.broadcasted_iota(jnp.int32, shape, 0) == row)


def hot_by_row(row, columns):
    count = row.shape[1]
    column = jnp.broadcast_to(row, (LANES, count)).T
    lane = lax.broadcasted_iota(jnp.int32, (count, LANES), 1)
    parts = [hot(column == lane + start) for start in range(0, columns, LANES)]
    return jnp.concatenate(parts, axis=1)


def fetch(sems, *pairs):
    copies = [pltpu.make_async_copy(src, dst, sems.at[i]) for i, (src, dst) in enumerate(pairs)]
    for copy in copies:
        copy.start()
    return copies


def join(ref, start, size):
    return jnp.concatenate([ref[q, start : start + size, :] for q in range(ref.shape[0])], axis=1)


def split_high_low(x):
    high = x.astype(BF16)
    return high, (x - high.astype(F32)).astype(BF16)


def first_kernel(node, rows, picked, node_here, rows_here, sems):
    copies = fetch(sems, (rows, rows_here), (node, node_here))
    copies[0].wait()
    pick = hot_by_row(rows_here[...], node.shape[0])
    copies[1].wait()
    picked[...] = mm(pick, node_here[...]).astype(BF16)


def spread_kernel(slot_rows, node, agg, spread):
    slots, count = slot_rows.shape[0], node.shape[0]
    for q in range(spread.shape[0]):
        spread[q, 0:slots, :] = slot_rows[...]
        spread[q, slots : slots + count, :] = node[...]
        spread[q, slots + count :, :] = agg[...]


def hidden_kernel(
    shared, edge_feat, w_send, w_recv, w_edge, w_out, receivers, slots, rows, spread
):
    edges, width = edge_feat.shape
    quarter = w_send.shape[1]
    slot_count = edges
    count = (shared.shape[1] - slot_count) // 2
    receive = hot_by_row(receivers[...], count)
    receiver_rows = mm(receive, join(shared, slot_count, count)).astype(BF16)
    message_grad = mm(receive, join(shared, slot_count + count, count)).astype(BF16)
    slot_hot = hot_by_row(slots[...], slot_count)
    sender_rows = mm(slot_hot, join(shared, 0, slot_count)).astype(BF16)
    rows[:, 0:width] = sender_rows
    rows[:, width : 2 * width] = receiver_rows
    rows[:, 2 * width : 3 * width] = message_grad
    act_grad = mm(message_grad, w_out[...])
    pre_act = (
        mm(sender_rows, w_send[...])
        + mm(receiver_rows, w_recv[...])
        + mm(edge_feat[...], w_edge[...])
    )
    gate = jax.nn.sigmoid(pre_act)
    rows[:, 3 * width :] = (pre_act * gate).astype(BF16)
    grad = (act_grad * gate * (1.0 + pre_act * (1.0 - gate))).astype(BF16)
    for q in range(spread.shape[0]):
        spread[q, 0:edges, :] = grad
        block = slice(q * quarter, (q + 1) * quarter)
        for i, weight in enumerate((w_send, w_recv, w_edge)):
            start = edges + i * quarter
            spread[q, start : start + quarter, :] = weight[block, :]


def weight_kernel(core, rows, edge_feat, spread, kept, given):
    edges, size = edge_feat.shape
    sender_rows, receiver_rows, message_grad = (
        rows[:, i * size : (i + 1) * size] for i in range(3)
    )
    grad = spread[0, 0:edges, :]
    mine = core[0] == 0
    for i, (low, high, high_right) in enumerate(
        (
            (sender_rows, edge_feat[...], grad),
            (receiver_rows, message_grad, rows[:, 3 * size :]),
        )
    ):
        low_sum = mm_tn(low, grad)
        high_sum = mm_tn(high, high_right)
        kept[i * size : (i + 1) * size, :] = jnp.where(mine, low_sum, high_sum)
        given[i * size : (i + 1) * size, :] = jnp.where(mine, high_sum, low_sum)


def payload_kernel(hidden, slots, kept, taken, payload):
    size = kept.shape[0] // 2
    quarter = kept.shape[1]
    edges = slots.shape[1]
    w_send = join(hidden, edges, quarter)
    sums = mm(hot_by_column(slots[...], payload.shape[0]), join(hidden, 0, edges))
    high, low = split_high_low(sums)
    payload[:, 0:quarter] = (kept[0:size, :] + taken[0:size, :]).astype(BF16)
    payload[:, quarter : 2 * quarter] = (kept[size:, :] + taken[size:, :]).astype(BF16)
    payload[:, 2 * quarter :] = (mm_nt(high, w_send) + mm_nt(low, w_send)).astype(BF16)


def edge_kernel(hidden, receivers, rows, edge_grad, recv_part, owner_hot):
    edges, quarter = edge_grad.shape
    full = join(hidden, 0, edges)
    edge_grad[...] = mm_nt(full, join(hidden, edges + 2 * quarter, quarter))
    sums = mm(hot_by_column(receivers[...], recv_part.shape[0]), full)
    high, low = split_high_low(sums)
    w_recv = join(hidden, edges + quarter, quarter)
    recv_part[...] = mm_nt(high, w_recv) + mm_nt(low, w_recv)
    owner_hot[...] = hot_by_column(rows[...], owner_hot.shape[0])


def last_kernel(
    arrived, owner_hot, recv_part, node_grad, grad_send, grad_recv, grad_edge, grad_out
):
    quarter = node_grad.shape[1]
    back = mm(owner_hot[...], arrived[:, 2 * quarter : 3 * quarter])
    node_grad[...] = recv_part[...] + back
    shape = (8, arrived.shape[0])
    place = lax.broadcasted_iota(jnp.int32, shape, 1) % 8
    pick = hot(place == lax.broadcasted_iota(jnp.int32, shape, 0))
    sums = mm(pick, arrived[:, 0 : 2 * quarter])
    grad_send[...] = sums[0:4, 0:quarter]
    grad_recv[...] = sums[0:4, quarter:]
    grad_edge[...] = sums[4:8, 0:quarter]
    grad_out[...] = sums[4:8, quarter:]


ANY = pl.BlockSpec(memory_space=pl.ANY)
VMEM = pl.BlockSpec(memory_space=pltpu.VMEM)
SMEM = pl.BlockSpec(memory_space=pltpu.SMEM)


def call(kernel, outs, *operands, places=None, scratch=(), flops=0, limit=24 * 1024 * 1024):
    moved = sum(x.size * x.dtype.itemsize for x in operands)
    moved += sum(x.size * x.dtype.itemsize for x in outs)
    return pl.pallas_call(
        kernel,
        out_shape=list(outs),
        in_specs=list(places or [VMEM] * len(operands)),
        out_specs=[VMEM] * len(outs),
        scratch_shapes=list(scratch),
        compiler_params=pltpu.CompilerParams(vmem_limit_bytes=limit),
        cost_estimate=pl.CostEstimate(flops=flops, bytes_accessed=moved, transcendentals=0),
    )(*operands)


def local(
    node, edge_feat, agg_grad, w_send, w_recv, w_edge, w_out, receivers, edge_slot, send_rows
):
    spaces = lax.axis_size("space")
    feats = lax.axis_size("feat")
    slot_count = send_rows.shape[1]
    capacity = slot_count // spaces
    node_count, quarter = node.shape
    edges, width = edge_feat.shape
    sds = jax.ShapeDtypeStruct
    receivers = receivers.reshape(1, edges)
    slots = edge_slot.reshape(1, edges)
    core = (lax.axis_index("space") % 2).reshape(1)

    def over_feat(x):
        return lax.all_to_all(x, "feat", split_axis=0, concat_axis=0, tiled=True)

    def over_space(x):
        lanes = x.shape[1]
        moved = lax.all_to_all(
            x.reshape(spaces, capacity, lanes), "space", split_axis=0, concat_axis=0, tiled=True
        )
        return moved.reshape(slot_count, lanes)

    (picked,) = call(
        first_kernel,
        (sds((slot_count, quarter), BF16),),
        node, send_rows,
        places=[ANY] * 2,
        scratch=[
            pltpu.VMEM(node.shape, BF16),
            pltpu.VMEM(send_rows.shape, jnp.int32),
            pltpu.SemaphoreType.DMA((2,)),
        ],
        flops=2 * slot_count * node_count * quarter,
        limit=60 * 1024 * 1024,
    )
    (spread,) = call(
        spread_kernel,
        (sds((feats, slot_count + 2 * node_count, quarter), BF16),),
        over_space(picked), node, agg_grad,
    )
    shared = over_feat(spread)
    rows, spread = call(
        hidden_kernel,
        (
            sds((edges, 3 * width + quarter), BF16),
            sds((feats, edges + 3 * quarter, quarter), BF16),
        ),
        shared, edge_feat, w_send, w_recv, w_edge, w_out, receivers, slots,
        flops=2 * edges * width * (2 * node_count + slot_count + 4 * quarter),
    )
    hidden = over_feat(spread)
    kept, given = call(
        weight_kernel,
        (sds((2 * width, quarter), F32), sds((2 * width, quarter), F32)),
        core, rows, edge_feat, spread,
        places=[SMEM] + [VMEM] * 3,
        flops=8 * edges * width * quarter,
    )
    taken = lax.ppermute(given, "space", [(i, i ^ 1) for i in range(spaces)])
    (payload,) = call(
        payload_kernel,
        (sds((slot_count, 3 * quarter), BF16),),
        hidden, slots, kept, taken,
        flops=2 * slot_count * width * (edges + 2 * quarter),
    )
    returned = over_space(payload)
    edge_grad, recv_part, owner_hot = call(
        edge_kernel,
        (
            sds((edges, quarter), F32),
            sds((node_count, quarter), F32),
            sds((node_count, slot_count), BF16),
        ),
        hidden, receivers, send_rows,
        flops=2 * edges * width * (node_count + 2 * quarter),
    )
    small = sds((width // spaces, quarter), F32)
    node_grad, grad_send, grad_recv, grad_edge, grad_out = call(
        last_kernel,
        (sds((node_count, quarter), F32), small, small, small, small),
        returned, owner_hot, recv_part,
        flops=2 * node_count * slot_count * quarter,
    )
    return (node_grad, edge_grad, grad_send, grad_recv, grad_edge, grad_out)


def solution(mesh):
    placed = (
        P("space", "feat"),
        P("space", None),
        P("space", "feat"),
        P(None, "feat"),
        P(None, "feat"),
        P(None, "feat"),
        P(None, "feat"),
        P("space"),
        P("space"),
        P("space", None),
    )
    return jax.shard_map(
        local,
        mesh=mesh,
        in_specs=placed,
        out_specs=(P("space", "feat"),) * 6,
        check_vma=False,
    )
```

```python
import jax
import jax.numpy as jnp
from jax import lax
from jax.experimental import pallas as pl
from jax.experimental.pallas import tpu as pltpu
from jax.sharding import PartitionSpec as P

F32 = jnp.float32
BF16 = jnp.bfloat16
LANES = 128
CAPACITY = 4


def mm(a, b):
    return jnp.dot(a, b, preferred_element_type=F32)


def mm_nt(a, b):
    return lax.dot_general(a, b, (((1,), (1,)), ((), ())), preferred_element_type=F32)


def mm_tn(a, b):
    return lax.dot_general(a, b, (((0,), (0,)), ((), ())), preferred_element_type=F32)


def hot(mask):
    return jnp.where(mask, 1.0, 0.0).astype(BF16)


def hot_by_column(row, rows):
    shape = (rows, row.shape[1])
    return hot(lax.broadcasted_iota(jnp.int32, shape, 0) == row)


def hot_by_row(row, columns):
    count = row.shape[1]
    column = jnp.broadcast_to(row, (LANES, count)).T
    lane = lax.broadcasted_iota(jnp.int32, (count, LANES), 1)
    parts = [hot(column == lane + start) for start in range(0, columns, LANES)]
    return jnp.concatenate(parts, axis=1)[:, 0:columns]


def fetch(sems, *pairs):
    copies = [pltpu.make_async_copy(src, dst, sems.at[i]) for i, (src, dst) in enumerate(pairs)]
    for copy in copies:
        copy.start()
    return copies


def join(ref, start, size):
    return jnp.concatenate([ref[q, start : start + size, :] for q in range(ref.shape[0])], axis=1)


def split_high_low(x):
    high = x.astype(BF16)
    return high, (x - high.astype(F32)).astype(BF16)


def pick_sum(hots, x):
    lanes = x.shape[1]
    both = mm(hots, jnp.concatenate(split_high_low(x), axis=1))
    return both[:, 0:lanes] + both[:, lanes:]


def high_low(product, a, x):
    high, low = split_high_low(x)
    return product(a, high) + product(a, low)


def first_kernel(node, rows, picked, node_here, rows_here, sems):
    copies = fetch(sems, (rows, rows_here), (node, node_here))
    copies[0].wait()
    pick = hot_by_row(rows_here[...], node.shape[0])
    copies[1].wait()
    picked[...] = mm(pick, node_here[...]).astype(BF16)


def early_kernel(region, node, agg, receivers, slots, send_rows, own, indices):
    count = node.shape[0]
    own[0:count, :] = node[...]
    own[count:, :] = agg[...]
    slot = slots[...]
    first = region[0] * CAPACITY
    lane = lax.broadcasted_iota(jnp.int32, send_rows.shape, 1)
    own_row = jnp.full(slot.shape, -1, jnp.int32)
    for k in range(CAPACITY):
        row = jnp.sum(jnp.where(lane == first + k, send_rows[...], 0), axis=1, keepdims=True)
        own_row = jnp.where(slot == first + k, row, own_row)
    other = jnp.where(slot >= first + CAPACITY, slot - CAPACITY, slot)
    other = jnp.where(own_row >= 0, -1, other)
    for i, values in enumerate((receivers[...], slot, other, own_row, send_rows[...])):
        indices[i : i + 1, :] = values


def pack_kernel(region, slot_rows, own, packed):
    start = own.shape[0]
    rest = packed.shape[0] - start
    rows = slot_rows[...].astype(F32)
    place = lax.broadcasted_iota(jnp.int32, (rest, rows.shape[1]), 0)
    kept = jnp.where(place < region[0] * CAPACITY, rows[0:rest, :], rows[CAPACITY:, :])
    packed[0:start, :] = own[...]
    packed[start:, :] = kept.astype(BF16)


def hidden_kernel(
    shared, edge_feat, w_send, w_recv, w_edge, w_out, indices, activation, spread
):
    edges, quarter = activation.shape
    slot_count = edges - CAPACITY
    count = (shared.shape[1] - slot_count) // 2
    at_node = mm(join(shared, 0, count), jnp.concatenate([w_recv[...], w_send[...]], axis=1))
    at_agg = mm(join(shared, count, count), w_out[...])
    at_slot = mm(join(shared, 2 * count, slot_count), w_send[...])
    receive = hot_by_row(indices[0:1, :], count)
    at_edge = pick_sum(receive, jnp.concatenate([at_node[:, 0:quarter], at_agg], axis=1))
    act_grad = at_edge[:, quarter:]
    pre_act = (
        pick_sum(hot_by_row(indices[2:3, :], slot_count), at_slot)
        + pick_sum(hot_by_row(indices[3:4, :], count), at_node[:, quarter:])
        + at_edge[:, 0:quarter]
        + mm(edge_feat[...], w_edge[...])
    )
    gate = jax.nn.sigmoid(pre_act)
    activation[...] = (pre_act * gate).astype(BF16)
    grad = (act_grad * gate * (1.0 + pre_act * (1.0 - gate))).astype(BF16)
    for q in range(spread.shape[0]):
        spread[q, 0:edges, :] = grad
        block = slice(q * quarter, (q + 1) * quarter)
        for i, weight in enumerate((w_send, w_recv, w_edge)):
            start = edges + i * quarter
            spread[q, start : start + quarter, :] = weight[block, :]


def weight_kernel(core, shared, edge_feat, indices, activation, spread, kept, given):
    edges, size = edge_feat.shape
    quarter = activation.shape[1]
    slot_count = edges - CAPACITY
    count = (shared.shape[1] - slot_count) // 2
    grad = spread[0, 0:edges, :]
    receive = hot_by_column(indices[0:1, :], count)
    by_slot = mm(hot_by_column(indices[2:3, :], slot_count), grad)
    by_own = mm(hot_by_column(indices[3:4, :], count), grad)
    by_node = mm(receive, grad)
    by_agg = mm(receive, activation[...])
    node_grads = high_low(
        mm_tn, join(shared, 0, count), jnp.concatenate([by_own, by_node], axis=1)
    )
    grads = (
        high_low(mm_tn, join(shared, 2 * count, slot_count), by_slot) + node_grads[:, 0:quarter],
        node_grads[:, quarter:],
        mm_tn(edge_feat[...], grad),
        high_low(mm_tn, join(shared, count, count), by_agg),
    )
    mine = core[0] == 0
    for i in range(2):
        kept[i * size : (i + 1) * size, :] = jnp.where(mine, grads[i], grads[i + 2])
        given[i * size : (i + 1) * size, :] = jnp.where(mine, grads[i + 2], grads[i])


def pair_kernel(kept, taken, sums):
    size = kept.shape[0] // 2
    quarter = kept.shape[1]
    for i in range(2):
        part = (kept[i * size : (i + 1) * size, :] + taken[i * size : (i + 1) * size, :]).astype(BF16)
        sums[:, :, i * quarter : (i + 1) * quarter] = part.reshape(*sums.shape[0:2], quarter)


def payload_kernel(hidden, indices, sums, payload):
    spaces, capacity, lanes = payload.shape
    quarter = hidden.shape[2]
    edges = indices.shape[1]
    payload[:, :, 0 : lanes - quarter] = sums[...]
    w_send = join(hidden, edges, quarter)
    terms = mm_nt(join(hidden, 0, edges), w_send)
    part = pick_sum(hot_by_column(indices[1:2, :], spaces * capacity), terms).astype(BF16)
    payload[:, :, lanes - quarter :] = part.reshape(spaces, capacity, quarter)


def edge_kernel(hidden, indices, edge_grad, recv_part, owner_hot):
    edges, quarter = edge_grad.shape
    full = join(hidden, 0, edges)
    edge_grad[...] = mm_nt(full, join(hidden, edges + 2 * quarter, quarter))
    terms = mm_nt(full, join(hidden, edges + quarter, quarter))
    recv_part[...] = pick_sum(hot_by_column(indices[0:1, :], recv_part.shape[0]), terms)
    owner_hot[...] = hot_by_column(indices[4:5, :], owner_hot.shape[0])


def last_kernel(
    arrived, owner_hot, recv_part, node_grad, grad_send, grad_recv, grad_edge, grad_out
):
    quarter = node_grad.shape[1]
    back = mm(owner_hot[...], arrived[:, 2 * quarter : 3 * quarter])
    node_grad[...] = recv_part[...] + back
    shape = (8, arrived.shape[0])
    place = lax.broadcasted_iota(jnp.int32, shape, 1) % 8
    pick = hot(place == lax.broadcasted_iota(jnp.int32, shape, 0))
    sums = mm(pick, arrived[:, 0 : 2 * quarter])
    grad_send[...] = sums[0:4, 0:quarter]
    grad_recv[...] = sums[0:4, quarter:]
    grad_edge[...] = sums[4:8, 0:quarter]
    grad_out[...] = sums[4:8, quarter:]


ANY = pl.BlockSpec(memory_space=pl.ANY)
VMEM = pl.BlockSpec(memory_space=pltpu.VMEM)
SMEM = pl.BlockSpec(memory_space=pltpu.SMEM)


def call(kernel, outs, *operands, places=None, scratch=(), flops=0, limit=24 * 1024 * 1024):
    moved = sum(x.size * x.dtype.itemsize for x in operands)
    moved += sum(x.size * x.dtype.itemsize for x in outs)
    return pl.pallas_call(
        kernel,
        out_shape=list(outs),
        in_specs=list(places or [VMEM] * len(operands)),
        out_specs=[VMEM] * len(outs),
        scratch_shapes=list(scratch),
        compiler_params=pltpu.CompilerParams(vmem_limit_bytes=limit),
        cost_estimate=pl.CostEstimate(flops=flops, bytes_accessed=moved, transcendentals=0),
    )(*operands)


def local(
    node, edge_feat, agg_grad, w_send, w_recv, w_edge, w_out, receivers, edge_slot, send_rows
):
    spaces = lax.axis_size("space")
    feats = lax.axis_size("feat")
    slot_count = send_rows.shape[1]
    capacity = slot_count // spaces
    node_count, quarter = node.shape
    edges, width = edge_feat.shape
    sds = jax.ShapeDtypeStruct
    receivers = receivers.reshape(1, edges)
    slots = edge_slot.reshape(1, edges)
    region = lax.axis_index("space").reshape(1)
    core = region % 2

    def over_feat(x):
        return lax.all_to_all(x, "feat", split_axis=0, concat_axis=0, tiled=True)

    def over_space(x):
        moved = lax.all_to_all(x, "space", split_axis=0, concat_axis=0, tiled=True)
        return moved.reshape(slot_count, x.shape[2])

    (picked,) = call(
        first_kernel,
        (sds((slot_count, quarter), BF16),),
        node, send_rows,
        places=[ANY] * 2,
        scratch=[
            pltpu.VMEM(node.shape, BF16),
            pltpu.VMEM(send_rows.shape, jnp.int32),
            pltpu.SemaphoreType.DMA((2,)),
        ],
        flops=2 * slot_count * node_count * quarter,
        limit=60 * 1024 * 1024,
    )
    own, indices = call(
        early_kernel,
        (sds((2 * node_count, quarter), BF16), sds((8, edges), jnp.int32)),
        region, node, agg_grad, receivers, slots, send_rows,
        places=[SMEM] + [VMEM] * 5,
    )
    (packed,) = call(
        pack_kernel,
        (sds((2 * node_count + slot_count - capacity, quarter), BF16),),
        region, over_space(picked.reshape(spaces, capacity, quarter)), own,
        places=[SMEM] + [VMEM] * 2,
    )
    shared = lax.all_gather(packed, "feat", axis=0, tiled=False)
    activation, spread = call(
        hidden_kernel,
        (
            sds((edges, quarter), BF16),
            sds((feats, edges + 3 * quarter, quarter), BF16),
        ),
        shared, edge_feat, w_send, w_recv, w_edge, w_out, indices,
        flops=2 * edges * width * (2 * node_count + slot_count + 4 * quarter),
    )
    hidden = over_feat(spread)
    kept, given = call(
        weight_kernel,
        (sds((2 * width, quarter), F32), sds((2 * width, quarter), F32)),
        core, shared, edge_feat, indices, activation, spread,
        places=[SMEM] + [VMEM] * 5,
        flops=8 * edges * width * quarter,
    )
    taken = lax.ppermute(given, "space", [(i, i ^ 1) for i in range(spaces)])
    (sums,) = call(pair_kernel, (sds((spaces, capacity, 2 * quarter), BF16),), kept, taken)
    (payload,) = call(
        payload_kernel,
        (sds((spaces, capacity, 3 * quarter), BF16),),
        hidden, indices, sums,
        flops=2 * slot_count * width * (edges + 2 * quarter),
    )
    returned = over_space(payload)
    edge_grad, recv_part, owner_hot = call(
        edge_kernel,
        (
            sds((edges, quarter), F32),
            sds((node_count, quarter), F32),
            sds((node_count, slot_count), BF16),
        ),
        hidden, indices,
        flops=2 * edges * width * (node_count + 2 * quarter),
    )
    small = sds((width // spaces, quarter), F32)
    node_grad, grad_send, grad_recv, grad_edge, grad_out = call(
        last_kernel,
        (sds((node_count, quarter), F32), small, small, small, small),
        returned, owner_hot, recv_part,
        flops=2 * node_count * slot_count * quarter,
    )
    return (node_grad, edge_grad, grad_send, grad_recv, grad_edge, grad_out)


def solution(mesh):
    placed = (
        P("space", "feat"),
        P("space", None),
        P("space", "feat"),
        P(None, "feat"),
        P(None, "feat"),
        P(None, "feat"),
        P(None, "feat"),
        P("space"),
        P("space"),
        P("space", None),
    )
    return jax.shard_map(
        local,
        mesh=mesh,
        in_specs=placed,
        out_specs=(P("space", "feat"),) * 6,
        check_vma=False,
    )
```

```python
import jax
import jax.numpy as jnp
from jax import lax
from jax.experimental import pallas as pl
from jax.experimental.pallas import tpu as pltpu
from jax.sharding import PartitionSpec as P

F32 = jnp.float32
BF16 = jnp.bfloat16
LANES = 128
CAPACITY = 4


def mm(a, b):
    return jnp.dot(a, b, preferred_element_type=F32)


def mm_nt(a, b):
    return lax.dot_general(a, b, (((1,), (1,)), ((), ())), preferred_element_type=F32)


def mm_tn(a, b):
    return lax.dot_general(a, b, (((0,), (0,)), ((), ())), preferred_element_type=F32)


def hot(mask):
    return jnp.where(mask, 1.0, 0.0).astype(BF16)


def hot_by_column(row, rows):
    shape = (rows, row.shape[1])
    return hot(lax.broadcasted_iota(jnp.int32, shape, 0) == row)


def hot_by_row(row, columns):
    count = row.shape[1]
    column = jnp.broadcast_to(row, (LANES, count)).T
    lane = lax.broadcasted_iota(jnp.int32, (count, LANES), 1)
    parts = [hot(column == lane + start) for start in range(0, columns, LANES)]
    return jnp.concatenate(parts, axis=1)[:, 0:columns]


def fetch(sems, *pairs):
    copies = [pltpu.make_async_copy(src, dst, sems.at[i]) for i, (src, dst) in enumerate(pairs)]
    for copy in copies:
        copy.start()
    return copies


def join(ref, start, size):
    return jnp.concatenate([ref[q, start : start + size, :] for q in range(ref.shape[0])], axis=1)


def split_high_low(x):
    high = x.astype(BF16)
    return high, (x - high.astype(F32)).astype(BF16)


def pick_sum(hots, x):
    lanes = x.shape[1]
    both = mm(hots, jnp.concatenate(split_high_low(x), axis=1))
    return both[:, 0:lanes] + both[:, lanes:]


def high_low(product, a, x):
    high, low = split_high_low(x)
    return product(a, high) + product(a, low)


def first_kernel(node, rows, picked, node_here, rows_here, sems):
    copies = fetch(sems, (rows, rows_here), (node, node_here))
    copies[0].wait()
    pick = hot_by_row(rows_here[...], node.shape[0])
    copies[1].wait()
    picked[...] = mm(pick, node_here[...]).astype(BF16)


def early_kernel(region, node, agg, receivers, slots, send_rows, own, indices):
    count = node.shape[0]
    own[0:count, :] = node[...]
    own[count:, :] = agg[...]
    slot = slots[...]
    first = region[0] * CAPACITY
    lane = lax.broadcasted_iota(jnp.int32, send_rows.shape, 1)
    own_row = jnp.full(slot.shape, -1, jnp.int32)
    for k in range(CAPACITY):
        row = jnp.sum(jnp.where(lane == first + k, send_rows[...], 0), axis=1, keepdims=True)
        own_row = jnp.where(slot == first + k, row, own_row)
    other = jnp.where(slot >= first + CAPACITY, slot - CAPACITY, slot)
    other = jnp.where(own_row >= 0, -1, other)
    for i, values in enumerate((receivers[...], slot, other, own_row, send_rows[...])):
        indices[i : i + 1, :] = values


def pack_kernel(region, slot_rows, own, packed):
    start = own.shape[0]
    rest = packed.shape[0] - start
    rows = slot_rows[...].astype(F32)
    place = lax.broadcasted_iota(jnp.int32, (rest, rows.shape[1]), 0)
    kept = jnp.where(place < region[0] * CAPACITY, rows[0:rest, :], rows[CAPACITY:, :])
    packed[0:start, :] = own[...]
    packed[start:, :] = kept.astype(BF16)


def hidden_kernel(
    shared, edge_feat, w_send, w_recv, w_edge, w_out, indices, activation, spread
):
    edges, quarter = activation.shape
    slot_count = edges - CAPACITY
    count = (shared.shape[1] - slot_count) // 2
    at_node = mm(join(shared, 0, count), jnp.concatenate([w_recv[...], w_send[...]], axis=1))
    at_agg = mm(join(shared, count, count), w_out[...])
    at_slot = mm(join(shared, 2 * count, slot_count), w_send[...])
    receive = hot_by_row(indices[0:1, :], count)
    at_edge = pick_sum(receive, jnp.concatenate([at_node[:, 0:quarter], at_agg], axis=1))
    act_grad = at_edge[:, quarter:]
    pre_act = (
        pick_sum(hot_by_row(indices[2:3, :], slot_count), at_slot)
        + pick_sum(hot_by_row(indices[3:4, :], count), at_node[:, quarter:])
        + at_edge[:, 0:quarter]
        + mm(edge_feat[...], w_edge[...])
    )
    gate = jax.nn.sigmoid(pre_act)
    activation[...] = (pre_act * gate).astype(BF16)
    grad = (act_grad * gate * (1.0 + pre_act * (1.0 - gate))).astype(BF16)
    for q in range(spread.shape[0]):
        spread[q, 0:edges, :] = grad
        block = slice(q * quarter, (q + 1) * quarter)
        for i, weight in enumerate((w_send, w_recv, w_edge)):
            start = edges + i * quarter
            spread[q, start : start + quarter, :] = weight[block, :]


def weight_kernel(core, shared, edge_feat, indices, activation, spread, kept, given):
    edges, size = edge_feat.shape
    quarter = activation.shape[1]
    slot_count = edges - CAPACITY
    count = (shared.shape[1] - slot_count) // 2
    grad = spread[0, 0:edges, :]
    receive = hot_by_column(indices[0:1, :], count)
    by_slot = mm(hot_by_column(indices[2:3, :], slot_count), grad)
    by_own = mm(hot_by_column(indices[3:4, :], count), grad)
    by_node = mm(receive, grad)
    by_agg = mm(receive, activation[...])
    node_grads = high_low(
        mm_tn, join(shared, 0, count), jnp.concatenate([by_own, by_node], axis=1)
    )
    grads = (
        high_low(mm_tn, join(shared, 2 * count, slot_count), by_slot) + node_grads[:, 0:quarter],
        node_grads[:, quarter:],
        mm_tn(edge_feat[...], grad),
        high_low(mm_tn, join(shared, count, count), by_agg),
    )
    mine = core[0] == 0
    for i in range(2):
        kept[i * size : (i + 1) * size, :] = jnp.where(mine, grads[i], grads[i + 2])
        given[i * size : (i + 1) * size, :] = jnp.where(mine, grads[i + 2], grads[i])


def pair_kernel(kept, taken, sums):
    size = kept.shape[0] // 2
    quarter = kept.shape[1]
    for i in range(2):
        part = (kept[i * size : (i + 1) * size, :] + taken[i * size : (i + 1) * size, :]).astype(BF16)
        sums[:, :, i * quarter : (i + 1) * quarter] = part.reshape(*sums.shape[0:2], quarter)


def payload_kernel(hidden, indices, sums, payload):
    spaces, capacity, lanes = payload.shape
    quarter = hidden.shape[2]
    edges = indices.shape[1]
    payload[:, :, 0 : lanes - quarter] = sums[...]
    w_send = join(hidden, edges, quarter)
    terms = mm_nt(join(hidden, 0, edges), w_send)
    part = pick_sum(hot_by_column(indices[1:2, :], spaces * capacity), terms).astype(BF16)
    payload[:, :, lanes - quarter :] = part.reshape(spaces, capacity, quarter)


def last_kernel(
    arrived, hidden, indices,
    edge_grad, node_grad, grad_send, grad_recv, grad_edge, grad_out, edge_here, sem,
):
    edges, quarter = edge_grad.shape
    full = join(hidden, 0, edges)
    edge_here[...] = mm_nt(full, join(hidden, edges + 2 * quarter, quarter))
    (copy,) = fetch(sem, (edge_here, edge_grad))
    terms = mm_nt(full, join(hidden, edges + quarter, quarter))
    count = node_grad.shape[0]
    node_grad[...] = pick_sum(hot_by_column(indices[0:1, :], count), terms) + mm(
        hot_by_column(indices[4:5, :], count), arrived[:, 2 * quarter : 3 * quarter]
    )
    shape = (8, arrived.shape[0])
    place = lax.broadcasted_iota(jnp.int32, shape, 1) % 8
    pick = hot(place == lax.broadcasted_iota(jnp.int32, shape, 0))
    sums = mm(pick, arrived[:, 0 : 2 * quarter])
    grad_send[...] = sums[0:4, 0:quarter]
    grad_recv[...] = sums[0:4, quarter:]
    grad_edge[...] = sums[4:8, 0:quarter]
    grad_out[...] = sums[4:8, quarter:]
    copy.wait()


ANY = pl.BlockSpec(memory_space=pl.ANY)
VMEM = pl.BlockSpec(memory_space=pltpu.VMEM)
SMEM = pl.BlockSpec(memory_space=pltpu.SMEM)


def call(kernel, outs, *operands, places=None, out_places=None, scratch=(), flops=0, limit=24 * 1024 * 1024):
    moved = sum(x.size * x.dtype.itemsize for x in operands)
    moved += sum(x.size * x.dtype.itemsize for x in outs)
    return pl.pallas_call(
        kernel,
        out_shape=list(outs),
        in_specs=list(places or [VMEM] * len(operands)),
        out_specs=list(out_places or [VMEM] * len(outs)),
        scratch_shapes=list(scratch),
        compiler_params=pltpu.CompilerParams(vmem_limit_bytes=limit),
        cost_estimate=pl.CostEstimate(flops=flops, bytes_accessed=moved, transcendentals=0),
    )(*operands)


def local(
    node, edge_feat, agg_grad, w_send, w_recv, w_edge, w_out, receivers, edge_slot, send_rows
):
    spaces = lax.axis_size("space")
    feats = lax.axis_size("feat")
    slot_count = send_rows.shape[1]
    capacity = slot_count // spaces
    node_count, quarter = node.shape
    edges, width = edge_feat.shape
    sds = jax.ShapeDtypeStruct
    receivers = receivers.reshape(1, edges)
    slots = edge_slot.reshape(1, edges)
    region = lax.axis_index("space").reshape(1)
    core = region % 2

    def over_feat(x):
        return lax.all_to_all(x, "feat", split_axis=0, concat_axis=0, tiled=True)

    def over_space(x):
        moved = lax.all_to_all(x, "space", split_axis=0, concat_axis=0, tiled=True)
        return moved.reshape(slot_count, x.shape[2])

    (picked,) = call(
        first_kernel,
        (sds((slot_count, quarter), BF16),),
        node, send_rows,
        places=[ANY] * 2,
        scratch=[
            pltpu.VMEM(node.shape, BF16),
            pltpu.VMEM(send_rows.shape, jnp.int32),
            pltpu.SemaphoreType.DMA((2,)),
        ],
        flops=2 * slot_count * node_count * quarter,
        limit=60 * 1024 * 1024,
    )
    own, indices = call(
        early_kernel,
        (sds((2 * node_count, quarter), BF16), sds((8, edges), jnp.int32)),
        region, node, agg_grad, receivers, slots, send_rows,
        places=[SMEM] + [VMEM] * 5,
    )
    (packed,) = call(
        pack_kernel,
        (sds((2 * node_count + slot_count - capacity, quarter), BF16),),
        region, over_space(picked.reshape(spaces, capacity, quarter)), own,
        places=[SMEM] + [VMEM] * 2,
    )
    shared = lax.all_gather(packed, "feat", axis=0, tiled=False)
    activation, spread = call(
        hidden_kernel,
        (
            sds((edges, quarter), BF16),
            sds((feats, edges + 3 * quarter, quarter), BF16),
        ),
        shared, edge_feat, w_send, w_recv, w_edge, w_out, indices,
        flops=2 * edges * width * (2 * node_count + slot_count + 4 * quarter),
    )
    hidden = over_feat(spread)
    kept, given = call(
        weight_kernel,
        (sds((2 * width, quarter), F32), sds((2 * width, quarter), F32)),
        core, shared, edge_feat, indices, activation, spread,
        places=[SMEM] + [VMEM] * 5,
        flops=8 * edges * width * quarter,
    )
    taken = lax.ppermute(given, "space", [(i, i ^ 1) for i in range(spaces)])
    (sums,) = call(pair_kernel, (sds((spaces, capacity, 2 * quarter), BF16),), kept, taken)
    (payload,) = call(
        payload_kernel,
        (sds((spaces, capacity, 3 * quarter), BF16),),
        hidden, indices, sums,
        flops=2 * slot_count * width * (edges + 2 * quarter),
    )
    returned = over_space(payload)
    small = sds((width // spaces, quarter), F32)
    edge_grad, node_grad, grad_send, grad_recv, grad_edge, grad_out = call(
        last_kernel,
        (
            sds((edges, quarter), F32),
            sds((node_count, quarter), F32),
            small, small, small, small,
        ),
        returned, hidden, indices,
        out_places=[ANY] + [VMEM] * 5,
        scratch=[pltpu.VMEM((edges, quarter), F32), pltpu.SemaphoreType.DMA((1,))],
        flops=2 * edges * (2 * width * quarter + 3 * node_count * quarter),
    )
    return (node_grad, edge_grad, grad_send, grad_recv, grad_edge, grad_out)


def solution(mesh):
    placed = (
        P("space", "feat"),
        P("space", None),
        P("space", "feat"),
        P(None, "feat"),
        P(None, "feat"),
        P(None, "feat"),
        P(None, "feat"),
        P("space"),
        P("space"),
        P("space", None),
    )
    return jax.shard_map(
        local,
        mesh=mesh,
        in_specs=placed,
        out_specs=(P("space", "feat"),) * 6,
        check_vma=False,
    )
```

```python
import functools

import jax
import jax.numpy as jnp
from jax import lax
from jax.experimental import pallas as pl
from jax.experimental.pallas import tpu as pltpu
from jax.sharding import PartitionSpec as P

F32 = jnp.float32
BF16 = jnp.bfloat16
LANES = 128
CAPACITY = 4
Z_STRIDE = 16


def mm(a, b):
    return jnp.dot(a, b, preferred_element_type=F32)


def mm_nt(a, b):
    return lax.dot_general(a, b, (((1,), (1,)), ((), ())), preferred_element_type=F32)


def mm_tn(a, b):
    return lax.dot_general(a, b, (((0,), (0,)), ((), ())), preferred_element_type=F32)


def hot(mask):
    return jnp.where(mask, 1.0, 0.0).astype(BF16)


def hot_by_column(row, rows):
    shape = (rows, row.shape[1])
    return hot(lax.broadcasted_iota(jnp.int32, shape, 0) == row)


def hot_by_row(row, columns):
    count = row.shape[1]
    column = jnp.broadcast_to(row, (LANES, count)).T
    lane = lax.broadcasted_iota(jnp.int32, (count, LANES), 1)
    parts = [hot(column == lane + start) for start in range(0, columns, LANES)]
    return jnp.concatenate(parts, axis=1)[:, 0:columns]


def fetch(sems, *pairs):
    copies = [pltpu.make_async_copy(src, dst, sems.at[i]) for i, (src, dst) in enumerate(pairs)]
    for copy in copies:
        copy.start()
    return copies


def join(ref, start, size):
    return jnp.concatenate([ref[q, start : start + size, :] for q in range(ref.shape[0])], axis=1)


def split_high_low(x):
    high = x.astype(BF16)
    return high, (x - high.astype(F32)).astype(BF16)


def pick_sum(hots, x):
    lanes = x.shape[1]
    both = mm(hots, jnp.concatenate(split_high_low(x), axis=1))
    return both[:, 0:lanes] + both[:, lanes:]


def high_low(product, a, x):
    high, low = split_high_low(x)
    return product(a, high) + product(a, low)


def first_kernel(node, rows, picked, node_here, rows_here, picked_here, sems, out_sems):
    copies = fetch(sems, (rows, rows_here), (node, node_here))
    copies[0].wait()
    picks = hot_by_row(rows_here[...], node.shape[0])
    copies[1].wait()
    size = picked.shape[0] // 2
    parts = []
    for i in range(2):
        part = pl.ds(i * size, size)
        picked_here[part, :] = mm(picks[i * size : (i + 1) * size], node_here[...]).astype(BF16)
        parts.append(
            pltpu.make_async_copy(picked_here.at[part, :], picked.at[part, :], out_sems.at[i])
        )
        parts[-1].start()
    for part in parts:
        part.wait()


def early_kernel(region, node, agg, receivers, slots, send_rows, own, indices):
    count = node.shape[0]
    own[0:count, :] = node[...]
    own[count:, :] = agg[...]
    slot = slots[...]
    first = region[0] * CAPACITY
    lane = lax.broadcasted_iota(jnp.int32, send_rows.shape, 1)
    own_row = jnp.full(slot.shape, -1, jnp.int32)
    for k in range(CAPACITY):
        row = jnp.sum(jnp.where(lane == first + k, send_rows[...], 0), axis=1, keepdims=True)
        own_row = jnp.where(slot == first + k, row, own_row)
    other = jnp.where(slot >= first + CAPACITY, slot - CAPACITY, slot)
    other = jnp.where(own_row >= 0, -1, other)
    for i, values in enumerate((receivers[...], slot, other, own_row, send_rows[...])):
        indices[i : i + 1, :] = values


def pack_kernel(region, slot_rows, own, packed):
    start = own.shape[0]
    rest = packed.shape[0] - start
    rows = slot_rows[...].astype(F32)
    place = lax.broadcasted_iota(jnp.int32, (rest, rows.shape[1]), 0)
    kept = jnp.where(place < region[0] * CAPACITY, rows[0:rest, :], rows[CAPACITY:, :])
    packed[0:start, :] = own[...]
    packed[start:, :] = kept.astype(BF16)


def hidden_kernel(
    shared, edge_feat, w_send, w_recv, w_edge, w_out, indices,
    activation, spread, hidden, sems, hidden_sems,
):
    edges, quarter = activation.shape
    feats = spread.shape[0]
    weights = (w_send, w_recv, w_edge)
    blocks = fetch(
        sems,
        *(
            (
                weight.at[q * quarter : (q + 1) * quarter, :],
                spread.at[q, edges + i * quarter : edges + (i + 1) * quarter, :],
            )
            for q in range(feats)
            for i, weight in enumerate(weights)
        ),
    )
    slot_count = edges - CAPACITY
    count = (shared.shape[1] - slot_count) // 2
    at_node = mm(join(shared, 0, count), jnp.concatenate([w_recv[...], w_send[...]], axis=1))
    at_agg = mm(join(shared, count, count), w_out[...])
    at_slot = mm(join(shared, 2 * count, slot_count), w_send[...])
    receive = hot_by_row(indices[0:1, :], count)
    at_edge = pick_sum(receive, jnp.concatenate([at_node[:, 0:quarter], at_agg], axis=1))
    act_grad = at_edge[:, quarter:]
    pre_act = (
        pick_sum(hot_by_row(indices[2:3, :], slot_count), at_slot)
        + pick_sum(hot_by_row(indices[3:4, :], count), at_node[:, quarter:])
        + at_edge[:, 0:quarter]
        + mm(edge_feat[...], w_edge[...])
    )
    gate = jax.nn.sigmoid(pre_act)
    activation[...] = (pre_act * gate).astype(BF16)
    hidden[...] = (act_grad * gate * (1.0 + pre_act * (1.0 - gate))).astype(BF16)
    rows = fetch(
        hidden_sems, *((hidden, spread.at[q, 0:edges, :]) for q in range(feats))
    )
    for copy in (*rows, *blocks):
        copy.wait()


def sender_grads(shared, indices, hidden, out):
    edges = hidden.shape[0]
    slot_count = edges - CAPACITY
    size = out.shape[0] // 2
    quarter = out.shape[1]
    count = (shared.shape[1] - slot_count) // 2
    grad = hidden[...]
    by_slot = mm(hot_by_column(indices[2:3, :], slot_count), grad)
    by_own = mm(hot_by_column(indices[3:4, :], count), grad)
    by_node = mm(hot_by_column(indices[0:1, :], count), grad)
    node_grads = high_low(
        mm_tn, join(shared, 0, count), jnp.concatenate([by_own, by_node], axis=1)
    )
    out[0:size, :] = (
        high_low(mm_tn, join(shared, 2 * count, slot_count), by_slot) + node_grads[:, 0:quarter]
    )
    out[size:, :] = node_grads[:, quarter:]


def edge_grads(shared, indices, hidden, edge_feat, activation, out):
    edges = hidden.shape[0]
    size = out.shape[0] // 2
    count = (shared.shape[1] - edges + CAPACITY) // 2
    out[0:size, :] = mm_tn(edge_feat[...], hidden[...])
    by_agg = mm(hot_by_column(indices[0:1, :], count), activation[...])
    out[size:, :] = high_low(mm_tn, join(shared, count, count), by_agg)


def weight_kernel(other, core, shared, edge_feat, indices, activation, hidden, out):
    first = (core[0] + other) % 2 == 0
    pl.when(first)(lambda: sender_grads(shared, indices, hidden, out))
    pl.when(jnp.logical_not(first))(
        lambda: edge_grads(shared, indices, hidden, edge_feat, activation, out)
    )


def pair_kernel(side, kept, taken, mine, given):
    size = mine.shape[0]
    first, second = (
        kept[i * size : (i + 1) * size, :] + taken[i * size : (i + 1) * size, :] for i in range(2)
    )
    even = side[0] == 0
    mine[...] = jnp.where(even, first, second)
    given[...] = jnp.where(even, second, first).astype(BF16)


def slot_kernel(hidden, indices, terms):
    spaces, capacity, quarter = terms.shape
    edges = indices.shape[1]
    w_send = join(hidden, edges, quarter)
    by_edge = mm_nt(join(hidden, 0, edges), w_send)
    sums = pick_sum(hot_by_column(indices[1:2, :], spaces * capacity), by_edge)
    terms[...] = sums.astype(BF16).reshape(terms.shape)


def payload_kernel(mine, taken, terms, payload):
    quarter = mine.shape[1]
    total = (mine[...] + taken[...].astype(F32)).astype(BF16)
    payload[:, :, 0:quarter] = total.reshape(terms.shape)
    payload[:, :, quarter:] = terms[...]


def last_kernel(
    arrived, hidden, indices,
    edge_grad, node_grad, grad_send, grad_recv, grad_edge, grad_out,
    edge_here, node_here, grads_here, sems,
):
    edges, quarter = edge_grad.shape
    full = join(hidden, 0, edges)
    edge_here[...] = mm_nt(full, join(hidden, edges + 2 * quarter, quarter))
    copies = fetch(sems, (edge_here, edge_grad))
    shape = (16, arrived.shape[0])
    place = lax.broadcasted_iota(jnp.int32, shape, 1)
    source = place // CAPACITY
    core = source % 2
    side = jnp.where(core == 0, source // 2, source // Z_STRIDE) % 2
    row = (2 * core + side) * CAPACITY + place % CAPACITY
    sums = mm(hot(row == lax.broadcasted_iota(jnp.int32, shape, 0)), arrived[:, 0:quarter])
    outs = (grad_send, grad_recv, grad_edge, grad_out)
    for i, out in enumerate(outs):
        grads_here[i] = sums[i * CAPACITY : (i + 1) * CAPACITY, :]
        copies += fetch(sems.at[1 + i : 2 + i], (grads_here.at[i], out))
    terms = mm_nt(full, join(hidden, edges + quarter, quarter))
    count = node_grad.shape[0]
    node_here[...] = pick_sum(hot_by_column(indices[0:1, :], count), terms) + mm(
        hot_by_column(indices[4:5, :], count), arrived[:, quarter:]
    )
    copies += fetch(sems.at[5:6], (node_here, node_grad))
    for copy in copies:
        copy.wait()


ANY = pl.BlockSpec(memory_space=pl.ANY)
VMEM = pl.BlockSpec(memory_space=pltpu.VMEM)
SMEM = pl.BlockSpec(memory_space=pltpu.SMEM)


def call(kernel, outs, *operands, places=None, out_places=None, scratch=(), flops=0, limit=24 * 1024 * 1024):
    moved = sum(x.size * x.dtype.itemsize for x in operands)
    moved += sum(x.size * x.dtype.itemsize for x in outs)
    return pl.pallas_call(
        kernel,
        out_shape=list(outs),
        in_specs=list(places or [VMEM] * len(operands)),
        out_specs=list(out_places or [VMEM] * len(outs)),
        scratch_shapes=list(scratch),
        compiler_params=pltpu.CompilerParams(vmem_limit_bytes=limit),
        cost_estimate=pl.CostEstimate(flops=flops, bytes_accessed=moved, transcendentals=0),
    )(*operands)


def local(
    node, edge_feat, agg_grad, w_send, w_recv, w_edge, w_out, receivers, edge_slot, send_rows
):
    spaces = lax.axis_size("space")
    feats = lax.axis_size("feat")
    slot_count = send_rows.shape[1]
    capacity = slot_count // spaces
    node_count, quarter = node.shape
    edges, width = edge_feat.shape
    sds = jax.ShapeDtypeStruct
    receivers = receivers.reshape(1, edges)
    slots = edge_slot.reshape(1, edges)
    region = lax.axis_index("space").reshape(1)
    core = region % 2

    def over_feat(x):
        return lax.all_to_all(x, "feat", split_axis=0, concat_axis=0, tiled=True)

    def over_space(x):
        moved = lax.all_to_all(x, "space", split_axis=0, concat_axis=0, tiled=True)
        return moved.reshape(slot_count, x.shape[2])

    (picked,) = call(
        first_kernel,
        (sds((slot_count, quarter), BF16),),
        node, send_rows,
        places=[ANY] * 2,
        scratch=[
            pltpu.VMEM(node.shape, BF16),
            pltpu.VMEM(send_rows.shape, jnp.int32),
            pltpu.VMEM((slot_count, quarter), BF16),
            pltpu.SemaphoreType.DMA((2,)),
            pltpu.SemaphoreType.DMA((2,)),
        ],
        out_places=[ANY],
        flops=2 * slot_count * node_count * quarter,
        limit=60 * 1024 * 1024,
    )
    own, indices = call(
        early_kernel,
        (sds((2 * node_count, quarter), BF16), sds((8, edges), jnp.int32)),
        region, node, agg_grad, receivers, slots, send_rows,
        places=[SMEM] + [VMEM] * 5,
    )
    (packed,) = call(
        pack_kernel,
        (sds((2 * node_count + slot_count - capacity, quarter), BF16),),
        region, over_space(picked.reshape(spaces, capacity, quarter)), own,
        places=[SMEM] + [VMEM] * 2,
    )
    shared = lax.all_gather(packed, "feat", axis=0, tiled=False)
    activation, spread, own_hidden = call(
        hidden_kernel,
        (
            sds((edges, quarter), BF16),
            sds((feats, edges + 3 * quarter, quarter), BF16),
            sds((edges, quarter), BF16),
        ),
        shared, edge_feat, w_send, w_recv, w_edge, w_out, indices,
        out_places=[VMEM, ANY, VMEM],
        scratch=[pltpu.SemaphoreType.DMA((3 * feats,)), pltpu.SemaphoreType.DMA((feats,))],
        flops=2 * edges * width * (2 * node_count + slot_count + 4 * quarter),
    )
    hidden = over_feat(spread)
    given, kept = (
        call(
            functools.partial(weight_kernel, other),
            (sds((2 * width, quarter), F32),),
            core, shared, edge_feat, indices, activation, own_hidden,
            places=[SMEM] + [VMEM] * 5,
            flops=4 * edges * width * quarter,
        )[0]
        for other in (1, 0)
    )
    taken = lax.ppermute(given, "space", [(i, i ^ 1) for i in range(spaces)])
    side = jnp.where(core == 0, region // 2, region // Z_STRIDE) % 2
    mine, given = call(
        pair_kernel,
        (sds((width, quarter), F32), sds((width, quarter), BF16)),
        side, kept, taken,
        places=[SMEM] + [VMEM] * 2,
    )
    taken = lax.ppermute(
        given, "space", [(i, i ^ (Z_STRIDE if i % 2 else 2)) for i in range(spaces)]
    )
    (terms,) = call(
        slot_kernel,
        (sds((spaces, capacity, quarter), BF16),),
        hidden, indices,
        flops=2 * edges * quarter * (width + 2 * slot_count),
    )
    (payload,) = call(
        payload_kernel, (sds((spaces, capacity, 2 * quarter), BF16),), mine, taken, terms
    )
    returned = over_space(payload)
    small = sds((width // spaces, quarter), F32)
    edge_grad, node_grad, grad_send, grad_recv, grad_edge, grad_out = call(
        last_kernel,
        (
            sds((edges, quarter), F32),
            sds((node_count, quarter), F32),
            small, small, small, small,
        ),
        returned, hidden, indices,
        out_places=[ANY] * 6,
        scratch=[
            pltpu.VMEM((edges, quarter), F32),
            pltpu.VMEM((node_count, quarter), F32),
            pltpu.VMEM((4, *small.shape), F32),
            pltpu.SemaphoreType.DMA((6,)),
        ],
        flops=2 * edges * (2 * width * quarter + 3 * node_count * quarter),
    )
    return (node_grad, edge_grad, grad_send, grad_recv, grad_edge, grad_out)


def solution(mesh):
    placed = (
        P("space", "feat"),
        P("space", None),
        P("space", "feat"),
        P(None, "feat"),
        P(None, "feat"),
        P(None, "feat"),
        P(None, "feat"),
        P("space"),
        P("space"),
        P("space", None),
    )
    return jax.shard_map(
        local,
        mesh=mesh,
        in_specs=placed,
        out_specs=(P("space", "feat"),) * 6,
        check_vma=False,
    )
```

```python
import functools

import jax
import jax.numpy as jnp
from jax import lax
from jax.experimental import pallas as pl
from jax.experimental.pallas import tpu as pltpu
from jax.sharding import PartitionSpec as P

F32 = jnp.float32
BF16 = jnp.bfloat16
LANES = 128
CAPACITY = 4
Z_STRIDE = 16


def mm(a, b):
    return jnp.dot(a, b, preferred_element_type=F32)


def mm_nt(a, b):
    return lax.dot_general(a, b, (((1,), (1,)), ((), ())), preferred_element_type=F32)


def mm_tn(a, b):
    return lax.dot_general(a, b, (((0,), (0,)), ((), ())), preferred_element_type=F32)


def hot(mask):
    return jnp.where(mask, 1.0, 0.0).astype(BF16)


def hot_by_column(row, rows):
    shape = (rows, row.shape[1])
    return hot(lax.broadcasted_iota(jnp.int32, shape, 0) == row)


def hot_by_row(row, columns):
    count = row.shape[1]
    column = jnp.broadcast_to(row, (LANES, count)).T
    lane = lax.broadcasted_iota(jnp.int32, (count, LANES), 1)
    parts = [hot(column == lane + start) for start in range(0, columns, LANES)]
    return jnp.concatenate(parts, axis=1)[:, 0:columns]


def fetch(sems, *pairs):
    copies = [pltpu.make_async_copy(src, dst, sems.at[i]) for i, (src, dst) in enumerate(pairs)]
    for copy in copies:
        copy.start()
    return copies


def join(ref, start, size):
    return jnp.concatenate([ref[q, start : start + size, :] for q in range(ref.shape[0])], axis=1)


def split_high_low(x):
    high = x.astype(BF16)
    return high, (x - high.astype(F32)).astype(BF16)


def pick_sum(hots, x):
    lanes = x.shape[1]
    both = mm(hots, jnp.concatenate(split_high_low(x), axis=1))
    return both[:, 0:lanes] + both[:, lanes:]


def high_low(product, a, x):
    high, low = split_high_low(x)
    return product(a, high) + product(a, low)


def first_kernel(node, rows, picked, node_here, rows_here, picked_here, sems, out_sems):
    copies = fetch(sems, (rows, rows_here), (node, node_here))
    copies[0].wait()
    picks = hot_by_row(rows_here[...], node.shape[0])
    copies[1].wait()
    size = picked.shape[0] // 2
    parts = []
    for i in range(2):
        part = pl.ds(i * size, size)
        picked_here[part, :] = mm(picks[i * size : (i + 1) * size], node_here[...]).astype(BF16)
        parts.append(
            pltpu.make_async_copy(picked_here.at[part, :], picked.at[part, :], out_sems.at[i])
        )
        parts[-1].start()
    for part in parts:
        part.wait()


def early_kernel(region, node, agg, receivers, slots, send_rows, own, indices):
    count = node.shape[0]
    own[0:count, :] = node[...]
    own[count:, :] = agg[...]
    slot = slots[...]
    first = region[0] * CAPACITY
    lane = lax.broadcasted_iota(jnp.int32, send_rows.shape, 1)
    own_row = jnp.full(slot.shape, -1, jnp.int32)
    for k in range(CAPACITY):
        row = jnp.sum(jnp.where(lane == first + k, send_rows[...], 0), axis=1, keepdims=True)
        own_row = jnp.where(slot == first + k, row, own_row)
    other = jnp.where(slot >= first + CAPACITY, slot - CAPACITY, slot)
    other = jnp.where(own_row >= 0, -1, other)
    for i, values in enumerate((receivers[...], slot, other, own_row, send_rows[...])):
        indices[i : i + 1, :] = values


def pack_kernel(region, slot_rows, own, packed):
    start = own.shape[0]
    rest = packed.shape[0] - start
    rows = slot_rows[...].astype(F32)
    place = lax.broadcasted_iota(jnp.int32, (rest, rows.shape[1]), 0)
    kept = jnp.where(place < region[0] * CAPACITY, rows[0:rest, :], rows[CAPACITY:, :])
    packed[0:start, :] = own[...]
    packed[start:, :] = kept.astype(BF16)


def hidden_kernel(
    shared, edge_feat, w_send, w_recv, w_edge, w_out, indices,
    activation, spread, hidden, sems, hidden_sems,
):
    edges, quarter = activation.shape
    feats = spread.shape[0]
    weights = (w_send, w_recv, w_edge)
    blocks = fetch(
        sems,
        *(
            (
                weight.at[q * quarter : (q + 1) * quarter, :],
                spread.at[q, edges + i * quarter : edges + (i + 1) * quarter, :],
            )
            for q in range(feats)
            for i, weight in enumerate(weights)
        ),
    )
    slot_count = edges - CAPACITY
    count = (shared.shape[1] - slot_count) // 2
    at_node = mm(join(shared, 0, count), jnp.concatenate([w_recv[...], w_send[...]], axis=1))
    at_agg = mm(join(shared, count, count), w_out[...])
    at_slot = mm(join(shared, 2 * count, slot_count), w_send[...])
    receive = hot_by_row(indices[0:1, :], count)
    at_edge = pick_sum(receive, jnp.concatenate([at_node[:, 0:quarter], at_agg], axis=1))
    act_grad = at_edge[:, quarter:]
    pre_act = (
        pick_sum(hot_by_row(indices[2:3, :], slot_count), at_slot)
        + pick_sum(hot_by_row(indices[3:4, :], count), at_node[:, quarter:])
        + at_edge[:, 0:quarter]
        + mm(edge_feat[...], w_edge[...])
    )
    gate = jax.nn.sigmoid(pre_act)
    activation[...] = (pre_act * gate).astype(BF16)
    hidden[...] = (act_grad * gate * (1.0 + pre_act * (1.0 - gate))).astype(BF16)
    rows = fetch(
        hidden_sems, *((hidden, spread.at[q, 0:edges, :]) for q in range(feats))
    )
    for copy in (*rows, *blocks):
        copy.wait()


def sender_grads(shared, indices, hidden, out):
    edges = hidden.shape[0]
    slot_count = edges - CAPACITY
    size = out.shape[0] // 2
    quarter = out.shape[1]
    count = (shared.shape[1] - slot_count) // 2
    grad = hidden[...]
    by_slot = mm(hot_by_column(indices[2:3, :], slot_count), grad)
    by_own = mm(hot_by_column(indices[3:4, :], count), grad)
    by_node = mm(hot_by_column(indices[0:1, :], count), grad)
    node_grads = high_low(
        mm_tn, join(shared, 0, count), jnp.concatenate([by_own, by_node], axis=1)
    )
    out[0:size, :] = (
        high_low(mm_tn, join(shared, 2 * count, slot_count), by_slot) + node_grads[:, 0:quarter]
    )
    out[size:, :] = node_grads[:, quarter:]


def edge_grads(shared, indices, hidden, edge_feat, activation, out):
    edges = hidden.shape[0]
    size = out.shape[0] // 2
    count = (shared.shape[1] - edges + CAPACITY) // 2
    out[0:size, :] = mm_tn(edge_feat[...], hidden[...])
    by_agg = mm(hot_by_column(indices[0:1, :], count), activation[...])
    out[size:, :] = high_low(mm_tn, join(shared, count, count), by_agg)


def weight_kernel(other, core, shared, edge_feat, indices, activation, hidden, out):
    first = (core[0] + other) % 2 == 0
    pl.when(first)(lambda: sender_grads(shared, indices, hidden, out))
    pl.when(jnp.logical_not(first))(
        lambda: edge_grads(shared, indices, hidden, edge_feat, activation, out)
    )


def pair_kernel(side, kept, taken, mine, given):
    size = mine.shape[0]
    first, second = (
        kept[i * size : (i + 1) * size, :] + taken[i * size : (i + 1) * size, :] for i in range(2)
    )
    even = side[0] == 0
    mine[...] = jnp.where(even, first, second)
    given[...] = jnp.where(even, second, first).astype(BF16)


def slot_kernel(hidden, indices, terms, edge_grad, recv_part, edge_here, sem):
    spaces, capacity, quarter = terms.shape
    edges = indices.shape[1]
    full = join(hidden, 0, edges)
    edge_here[...] = mm_nt(full, join(hidden, edges + 2 * quarter, quarter))
    (copy,) = fetch(sem, (edge_here, edge_grad))
    by_edge = mm_nt(full, join(hidden, edges, quarter))
    sums = pick_sum(hot_by_column(indices[1:2, :], spaces * capacity), by_edge)
    terms[...] = sums.astype(BF16).reshape(terms.shape)
    by_edge = mm_nt(full, join(hidden, edges + quarter, quarter))
    recv_part[...] = pick_sum(hot_by_column(indices[0:1, :], recv_part.shape[0]), by_edge)
    copy.wait()


def payload_kernel(mine, taken, terms, payload):
    quarter = mine.shape[1]
    total = (mine[...] + taken[...].astype(F32)).astype(BF16)
    payload[:, :, 0:quarter] = total.reshape(terms.shape)
    payload[:, :, quarter:] = terms[...]


def last_kernel(
    arrived, indices, recv_part,
    node_grad, grad_send, grad_recv, grad_edge, grad_out, node_here, grads_here, sems,
):
    count, quarter = node_grad.shape
    back = mm(hot_by_column(indices[4:5, :], count), arrived[:, quarter:])
    node_here[...] = recv_part[...] + back
    copies = fetch(sems.at[4:5], (node_here, node_grad))
    shape = (16, arrived.shape[0])
    place = lax.broadcasted_iota(jnp.int32, shape, 1)
    source = place // CAPACITY
    core = source % 2
    side = jnp.where(core == 0, source // 2, source // Z_STRIDE) % 2
    row = (2 * core + side) * CAPACITY + place % CAPACITY
    sums = mm(hot(row == lax.broadcasted_iota(jnp.int32, shape, 0)), arrived[:, 0:quarter])
    outs = (grad_send, grad_recv, grad_edge, grad_out)
    for i, out in enumerate(outs):
        grads_here[i] = sums[i * CAPACITY : (i + 1) * CAPACITY, :]
        copies += fetch(sems.at[i : i + 1], (grads_here.at[i], out))
    for copy in copies:
        copy.wait()


ANY = pl.BlockSpec(memory_space=pl.ANY)
VMEM = pl.BlockSpec(memory_space=pltpu.VMEM)
SMEM = pl.BlockSpec(memory_space=pltpu.SMEM)


def call(kernel, outs, *operands, places=None, out_places=None, scratch=(), flops=0, limit=24 * 1024 * 1024):
    moved = sum(x.size * x.dtype.itemsize for x in operands)
    moved += sum(x.size * x.dtype.itemsize for x in outs)
    return pl.pallas_call(
        kernel,
        out_shape=list(outs),
        in_specs=list(places or [VMEM] * len(operands)),
        out_specs=list(out_places or [VMEM] * len(outs)),
        scratch_shapes=list(scratch),
        compiler_params=pltpu.CompilerParams(vmem_limit_bytes=limit),
        cost_estimate=pl.CostEstimate(flops=flops, bytes_accessed=moved, transcendentals=0),
    )(*operands)


def local(
    node, edge_feat, agg_grad, w_send, w_recv, w_edge, w_out, receivers, edge_slot, send_rows
):
    spaces = lax.axis_size("space")
    feats = lax.axis_size("feat")
    slot_count = send_rows.shape[1]
    capacity = slot_count // spaces
    node_count, quarter = node.shape
    edges, width = edge_feat.shape
    sds = jax.ShapeDtypeStruct
    receivers = receivers.reshape(1, edges)
    slots = edge_slot.reshape(1, edges)
    region = lax.axis_index("space").reshape(1)
    core = region % 2

    def over_feat(x):
        return lax.all_to_all(x, "feat", split_axis=0, concat_axis=0, tiled=True)

    def over_space(x):
        moved = lax.all_to_all(x, "space", split_axis=0, concat_axis=0, tiled=True)
        return moved.reshape(slot_count, x.shape[2])

    (picked,) = call(
        first_kernel,
        (sds((slot_count, quarter), BF16),),
        node, send_rows,
        places=[ANY] * 2,
        scratch=[
            pltpu.VMEM(node.shape, BF16),
            pltpu.VMEM(send_rows.shape, jnp.int32),
            pltpu.VMEM((slot_count, quarter), BF16),
            pltpu.SemaphoreType.DMA((2,)),
            pltpu.SemaphoreType.DMA((2,)),
        ],
        out_places=[ANY],
        flops=2 * slot_count * node_count * quarter,
        limit=60 * 1024 * 1024,
    )
    own, indices = call(
        early_kernel,
        (sds((2 * node_count, quarter), BF16), sds((8, edges), jnp.int32)),
        region, node, agg_grad, receivers, slots, send_rows,
        places=[SMEM] + [VMEM] * 5,
    )
    (packed,) = call(
        pack_kernel,
        (sds((2 * node_count + slot_count - capacity, quarter), BF16),),
        region, over_space(picked.reshape(spaces, capacity, quarter)), own,
        places=[SMEM] + [VMEM] * 2,
    )
    shared = lax.all_gather(packed, "feat", axis=0, tiled=False)
    activation, spread, own_hidden = call(
        hidden_kernel,
        (
            sds((edges, quarter), BF16),
            sds((feats, edges + 3 * quarter, quarter), BF16),
            sds((edges, quarter), BF16),
        ),
        shared, edge_feat, w_send, w_recv, w_edge, w_out, indices,
        out_places=[VMEM, ANY, VMEM],
        scratch=[pltpu.SemaphoreType.DMA((3 * feats,)), pltpu.SemaphoreType.DMA((feats,))],
        flops=2 * edges * width * (2 * node_count + slot_count + 4 * quarter),
    )
    hidden = over_feat(spread)
    given, kept = (
        call(
            functools.partial(weight_kernel, other),
            (sds((2 * width, quarter), F32),),
            core, shared, edge_feat, indices, activation, own_hidden,
            places=[SMEM] + [VMEM] * 5,
            flops=4 * edges * width * quarter,
        )[0]
        for other in (1, 0)
    )
    taken = lax.ppermute(given, "space", [(i, i ^ 1) for i in range(spaces)])
    side = jnp.where(core == 0, region // 2, region // Z_STRIDE) % 2
    mine, given = call(
        pair_kernel,
        (sds((width, quarter), F32), sds((width, quarter), BF16)),
        side, kept, taken,
        places=[SMEM] + [VMEM] * 2,
    )
    taken = lax.ppermute(
        given, "space", [(i, i ^ (Z_STRIDE if i % 2 else 2)) for i in range(spaces)]
    )
    terms, edge_grad, recv_part = call(
        slot_kernel,
        (
            sds((spaces, capacity, quarter), BF16),
            sds((edges, quarter), F32),
            sds((node_count, quarter), F32),
        ),
        hidden, indices,
        out_places=[VMEM, ANY, VMEM],
        scratch=[pltpu.VMEM((edges, quarter), F32), pltpu.SemaphoreType.DMA((1,))],
        flops=2 * edges * quarter * (3 * width + 2 * slot_count + 2 * node_count),
    )
    (payload,) = call(
        payload_kernel, (sds((spaces, capacity, 2 * quarter), BF16),), mine, taken, terms
    )
    returned = over_space(payload)
    small = sds((width // spaces, quarter), F32)
    node_grad, grad_send, grad_recv, grad_edge, grad_out = call(
        last_kernel,
        (sds((node_count, quarter), F32), small, small, small, small),
        returned, indices, recv_part,
        out_places=[ANY] * 5,
        scratch=[
            pltpu.VMEM((node_count, quarter), F32),
            pltpu.VMEM((4, *small.shape), F32),
            pltpu.SemaphoreType.DMA((5,)),
        ],
        flops=2 * slot_count * quarter * (node_count + 16),
    )
    return (node_grad, edge_grad, grad_send, grad_recv, grad_edge, grad_out)


def solution(mesh):
    placed = (
        P("space", "feat"),
        P("space", None),
        P("space", "feat"),
        P(None, "feat"),
        P(None, "feat"),
        P(None, "feat"),
        P(None, "feat"),
        P("space"),
        P("space"),
        P("space", None),
    )
    return jax.shard_map(
        local,
        mesh=mesh,
        in_specs=placed,
        out_specs=(P("space", "feat"),) * 6,
        check_vma=False,
    )
```

```python
import functools

import jax
import jax.numpy as jnp
from jax import lax
from jax.experimental import pallas as pl
from jax.experimental.pallas import tpu as pltpu
from jax.sharding import PartitionSpec as P

F32 = jnp.float32
BF16 = jnp.bfloat16
LANES = 128
CAPACITY = 4
Z_STRIDE = 16


def mm(a, b):
    return jnp.dot(a, b, preferred_element_type=F32)


def mm_nt(a, b):
    return lax.dot_general(a, b, (((1,), (1,)), ((), ())), preferred_element_type=F32)


def mm_tn(a, b):
    return lax.dot_general(a, b, (((0,), (0,)), ((), ())), preferred_element_type=F32)


def hot(mask):
    return jnp.where(mask, 1.0, 0.0).astype(BF16)


def hot_by_column(row, rows):
    shape = (rows, row.shape[1])
    return hot(lax.broadcasted_iota(jnp.int32, shape, 0) == row)


def hot_by_row(row, columns):
    count = row.shape[1]
    column = jnp.broadcast_to(row, (LANES, count)).T
    lane = lax.broadcasted_iota(jnp.int32, (count, LANES), 1)
    parts = [hot(column == lane + start) for start in range(0, columns, LANES)]
    return jnp.concatenate(parts, axis=1)[:, 0:columns]


def fetch(sems, *pairs):
    copies = [pltpu.make_async_copy(src, dst, sems.at[i]) for i, (src, dst) in enumerate(pairs)]
    for copy in copies:
        copy.start()
    return copies


def join(ref, start, size):
    return jnp.concatenate([ref[q, start : start + size, :] for q in range(ref.shape[0])], axis=1)


def split_high_low(x):
    high = x.astype(BF16)
    return high, (x - high.astype(F32)).astype(BF16)


def pick_sum(hots, x):
    lanes = x.shape[1]
    both = mm(hots, jnp.concatenate(split_high_low(x), axis=1))
    return both[:, 0:lanes] + both[:, lanes:]


def high_low(product, a, x):
    high, low = split_high_low(x)
    return product(a, high) + product(a, low)


def first_kernel(node, rows, picked, node_here, rows_here, picked_here, sems, out_sems):
    copies = fetch(sems, (rows, rows_here), (node, node_here))
    copies[0].wait()
    picks = hot_by_row(rows_here[...], node.shape[0])
    copies[1].wait()
    size = picked.shape[0] // 2
    parts = []
    for i in range(2):
        part = pl.ds(i * size, size)
        picked_here[part, :] = mm(picks[i * size : (i + 1) * size], node_here[...]).astype(BF16)
        parts.append(
            pltpu.make_async_copy(picked_here.at[part, :], picked.at[part, :], out_sems.at[i])
        )
        parts[-1].start()
    for part in parts:
        part.wait()


def early_kernel(region, node, agg, receivers, slots, send_rows, own, indices):
    count = node.shape[0]
    own[0:count, :] = node[...]
    own[count:, :] = agg[...]
    slot = slots[...]
    first = region[0] * CAPACITY
    lane = lax.broadcasted_iota(jnp.int32, send_rows.shape, 1)
    own_row = jnp.full(slot.shape, -1, jnp.int32)
    for k in range(CAPACITY):
        row = jnp.sum(jnp.where(lane == first + k, send_rows[...], 0), axis=1, keepdims=True)
        own_row = jnp.where(slot == first + k, row, own_row)
    other = jnp.where(slot >= first + CAPACITY, slot - CAPACITY, slot)
    other = jnp.where(own_row >= 0, -1, other)
    for i, values in enumerate((receivers[...], slot, other, own_row, send_rows[...])):
        indices[i : i + 1, :] = values


def pack_kernel(region, slot_rows, own, packed):
    start = own.shape[0]
    rest = packed.shape[0] - start
    rows = slot_rows[...].astype(F32)
    place = lax.broadcasted_iota(jnp.int32, (rest, rows.shape[1]), 0)
    kept = jnp.where(place < region[0] * CAPACITY, rows[0:rest, :], rows[CAPACITY:, :])
    packed[0:start, :] = own[...]
    packed[start:, :] = kept.astype(BF16)


def hidden_kernel(
    shared, edge_feat, w_send, w_recv, w_edge, w_out, indices,
    activation, spread, hidden, sems, hidden_sems,
):
    edges, quarter = activation.shape
    feats = spread.shape[0]
    weights = (w_send, w_recv, w_edge)
    blocks = fetch(
        sems,
        *(
            (
                weight.at[q * quarter : (q + 1) * quarter, :],
                spread.at[q, edges + i * quarter : edges + (i + 1) * quarter, :],
            )
            for q in range(feats)
            for i, weight in enumerate(weights)
        ),
    )
    slot_count = edges - CAPACITY
    count = (shared.shape[1] - slot_count) // 2
    at_node = mm(join(shared, 0, count), jnp.concatenate([w_recv[...], w_send[...]], axis=1))
    at_agg = mm(join(shared, count, count), w_out[...])
    at_slot = mm(join(shared, 2 * count, slot_count), w_send[...])
    at_row = jnp.concatenate([at_node[:, 0:quarter], at_agg], axis=1)
    size = edges // 2
    rows = []
    for half in range(2):
        part = slice(half * size, (half + 1) * size)
        at_edge = pick_sum(hot_by_row(indices[0:1, part], count), at_row)
        act_grad = at_edge[:, quarter:]
        pre_act = (
            pick_sum(hot_by_row(indices[2:3, part], slot_count), at_slot)
            + pick_sum(hot_by_row(indices[3:4, part], count), at_node[:, quarter:])
            + at_edge[:, 0:quarter]
            + mm(edge_feat[part, :], w_edge[...])
        )
        gate = jax.nn.sigmoid(pre_act)
        hidden[part, :] = (act_grad * gate * (1.0 + pre_act * (1.0 - gate))).astype(BF16)
        rows += fetch(
            hidden_sems.at[half * feats : (half + 1) * feats],
            *((hidden.at[part, :], spread.at[q, part, :]) for q in range(feats)),
        )
        activation[part, :] = (pre_act * gate).astype(BF16)
    for copy in (*rows, *blocks):
        copy.wait()


def sender_grads(shared, indices, hidden, out):
    edges = hidden.shape[0]
    slot_count = edges - CAPACITY
    size = out.shape[0] // 2
    quarter = out.shape[1]
    count = (shared.shape[1] - slot_count) // 2
    grad = hidden[...]
    by_slot = mm(hot_by_column(indices[2:3, :], slot_count), grad)
    by_own = mm(hot_by_column(indices[3:4, :], count), grad)
    by_node = mm(hot_by_column(indices[0:1, :], count), grad)
    node_grads = high_low(
        mm_tn, join(shared, 0, count), jnp.concatenate([by_own, by_node], axis=1)
    )
    out[0:size, :] = (
        high_low(mm_tn, join(shared, 2 * count, slot_count), by_slot) + node_grads[:, 0:quarter]
    )
    out[size:, :] = node_grads[:, quarter:]


def edge_grads(shared, indices, hidden, edge_feat, activation, out):
    edges = hidden.shape[0]
    size = out.shape[0] // 2
    count = (shared.shape[1] - edges + CAPACITY) // 2
    out[0:size, :] = mm_tn(edge_feat[...], hidden[...])
    by_agg = mm(hot_by_column(indices[0:1, :], count), activation[...])
    out[size:, :] = high_low(mm_tn, join(shared, count, count), by_agg)


def weight_kernel(other, core, shared, edge_feat, indices, activation, hidden, out):
    first = (core[0] + other) % 2 == 0
    pl.when(first)(lambda: sender_grads(shared, indices, hidden, out))
    pl.when(jnp.logical_not(first))(
        lambda: edge_grads(shared, indices, hidden, edge_feat, activation, out)
    )


def pair_kernel(side, kept, taken, mine, given):
    size = mine.shape[0]
    first, second = (
        kept[i * size : (i + 1) * size, :] + taken[i * size : (i + 1) * size, :] for i in range(2)
    )
    even = side[0] == 0
    mine[...] = jnp.where(even, first, second)
    given[...] = jnp.where(even, second, first).astype(BF16)


def slot_kernel(hidden, indices, terms):
    spaces, capacity, quarter = terms.shape
    edges = indices.shape[1]
    w_send = join(hidden, edges, quarter)
    by_edge = mm_nt(join(hidden, 0, edges), w_send)
    sums = pick_sum(hot_by_column(indices[1:2, :], spaces * capacity), by_edge)
    terms[...] = sums.astype(BF16).reshape(terms.shape)


def payload_kernel(mine, taken, terms, payload):
    quarter = mine.shape[1]
    total = (mine[...] + taken[...].astype(F32)).astype(BF16)
    payload[:, :, 0:quarter] = total.reshape(terms.shape)
    payload[:, :, quarter:] = terms[...]


def last_kernel(
    arrived, hidden, indices,
    edge_grad, node_grad, grad_send, grad_recv, grad_edge, grad_out,
    edge_here, node_here, grads_here, sems,
):
    edges, quarter = edge_grad.shape
    full = join(hidden, 0, edges)
    edge_here[...] = mm_nt(full, join(hidden, edges + 2 * quarter, quarter))
    copies = fetch(sems, (edge_here, edge_grad))
    shape = (16, arrived.shape[0])
    place = lax.broadcasted_iota(jnp.int32, shape, 1)
    source = place // CAPACITY
    core = source % 2
    side = jnp.where(core == 0, source // 2, source // Z_STRIDE) % 2
    row = (2 * core + side) * CAPACITY + place % CAPACITY
    sums = mm(hot(row == lax.broadcasted_iota(jnp.int32, shape, 0)), arrived[:, 0:quarter])
    outs = (grad_send, grad_recv, grad_edge, grad_out)
    for i, out in enumerate(outs):
        grads_here[i] = sums[i * CAPACITY : (i + 1) * CAPACITY, :]
        copies += fetch(sems.at[1 + i : 2 + i], (grads_here.at[i], out))
    terms = mm_nt(full, join(hidden, edges + quarter, quarter))
    count = node_grad.shape[0]
    node_here[...] = pick_sum(hot_by_column(indices[0:1, :], count), terms) + mm(
        hot_by_column(indices[4:5, :], count), arrived[:, quarter:]
    )
    copies += fetch(sems.at[5:6], (node_here, node_grad))
    for copy in copies:
        copy.wait()


ANY = pl.BlockSpec(memory_space=pl.ANY)
VMEM = pl.BlockSpec(memory_space=pltpu.VMEM)
SMEM = pl.BlockSpec(memory_space=pltpu.SMEM)


def call(kernel, outs, *operands, places=None, out_places=None, scratch=(), flops=0, limit=24 * 1024 * 1024):
    moved = sum(x.size * x.dtype.itemsize for x in operands)
    moved += sum(x.size * x.dtype.itemsize for x in outs)
    return pl.pallas_call(
        kernel,
        out_shape=list(outs),
        in_specs=list(places or [VMEM] * len(operands)),
        out_specs=list(out_places or [VMEM] * len(outs)),
        scratch_shapes=list(scratch),
        compiler_params=pltpu.CompilerParams(vmem_limit_bytes=limit),
        cost_estimate=pl.CostEstimate(flops=flops, bytes_accessed=moved, transcendentals=0),
    )(*operands)


def local(
    node, edge_feat, agg_grad, w_send, w_recv, w_edge, w_out, receivers, edge_slot, send_rows
):
    spaces = lax.axis_size("space")
    feats = lax.axis_size("feat")
    slot_count = send_rows.shape[1]
    capacity = slot_count // spaces
    node_count, quarter = node.shape
    edges, width = edge_feat.shape
    sds = jax.ShapeDtypeStruct
    receivers = receivers.reshape(1, edges)
    slots = edge_slot.reshape(1, edges)
    region = lax.axis_index("space").reshape(1)
    core = region % 2

    def over_feat(x):
        return lax.all_to_all(x, "feat", split_axis=0, concat_axis=0, tiled=True)

    def over_space(x):
        moved = lax.all_to_all(x, "space", split_axis=0, concat_axis=0, tiled=True)
        return moved.reshape(slot_count, x.shape[2])

    (picked,) = call(
        first_kernel,
        (sds((slot_count, quarter), BF16),),
        node, send_rows,
        places=[ANY] * 2,
        scratch=[
            pltpu.VMEM(node.shape, BF16),
            pltpu.VMEM(send_rows.shape, jnp.int32),
            pltpu.VMEM((slot_count, quarter), BF16),
            pltpu.SemaphoreType.DMA((2,)),
            pltpu.SemaphoreType.DMA((2,)),
        ],
        out_places=[ANY],
        flops=2 * slot_count * node_count * quarter,
        limit=60 * 1024 * 1024,
    )
    own, indices = call(
        early_kernel,
        (sds((2 * node_count, quarter), BF16), sds((8, edges), jnp.int32)),
        region, node, agg_grad, receivers, slots, send_rows,
        places=[SMEM] + [VMEM] * 5,
    )
    (packed,) = call(
        pack_kernel,
        (sds((2 * node_count + slot_count - capacity, quarter), BF16),),
        region, over_space(picked.reshape(spaces, capacity, quarter)), own,
        places=[SMEM] + [VMEM] * 2,
    )
    shared = lax.all_gather(packed, "feat", axis=0, tiled=False)
    activation, spread, own_hidden = call(
        hidden_kernel,
        (
            sds((edges, quarter), BF16),
            sds((feats, edges + 3 * quarter, quarter), BF16),
            sds((edges, quarter), BF16),
        ),
        shared, edge_feat, w_send, w_recv, w_edge, w_out, indices,
        out_places=[VMEM, ANY, VMEM],
        scratch=[pltpu.SemaphoreType.DMA((3 * feats,)), pltpu.SemaphoreType.DMA((2 * feats,))],
        flops=2 * edges * width * (2 * node_count + slot_count + 4 * quarter),
    )
    hidden = over_feat(spread)
    given, kept = (
        call(
            functools.partial(weight_kernel, other),
            (sds((2 * width, quarter), F32),),
            core, shared, edge_feat, indices, activation, own_hidden,
            places=[SMEM] + [VMEM] * 5,
            flops=4 * edges * width * quarter,
        )[0]
        for other in (1, 0)
    )
    taken = lax.ppermute(given, "space", [(i, i ^ 1) for i in range(spaces)])
    side = jnp.where(core == 0, region // 2, region // Z_STRIDE) % 2
    mine, given = call(
        pair_kernel,
        (sds((width, quarter), F32), sds((width, quarter), BF16)),
        side, kept, taken,
        places=[SMEM] + [VMEM] * 2,
    )
    taken = lax.ppermute(
        given, "space", [(i, i ^ (Z_STRIDE if i % 2 else 2)) for i in range(spaces)]
    )
    (terms,) = call(
        slot_kernel,
        (sds((spaces, capacity, quarter), BF16),),
        hidden, indices,
        flops=2 * edges * quarter * (width + 2 * slot_count),
    )
    (payload,) = call(
        payload_kernel, (sds((spaces, capacity, 2 * quarter), BF16),), mine, taken, terms
    )
    returned = over_space(payload)
    small = sds((width // spaces, quarter), F32)
    edge_grad, node_grad, grad_send, grad_recv, grad_edge, grad_out = call(
        last_kernel,
        (
            sds((edges, quarter), F32),
            sds((node_count, quarter), F32),
            small, small, small, small,
        ),
        returned, hidden, indices,
        out_places=[ANY] * 6,
        scratch=[
            pltpu.VMEM((edges, quarter), F32),
            pltpu.VMEM((node_count, quarter), F32),
            pltpu.VMEM((4, *small.shape), F32),
            pltpu.SemaphoreType.DMA((6,)),
        ],
        flops=2 * edges * (2 * width * quarter + 3 * node_count * quarter),
    )
    return (node_grad, edge_grad, grad_send, grad_recv, grad_edge, grad_out)


def solution(mesh):
    placed = (
        P("space", "feat"),
        P("space", None),
        P("space", "feat"),
        P(None, "feat"),
        P(None, "feat"),
        P(None, "feat"),
        P(None, "feat"),
        P("space"),
        P("space"),
        P("space", None),
    )
    return jax.shard_map(
        local,
        mesh=mesh,
        in_specs=placed,
        out_specs=(P("space", "feat"),) * 6,
        check_vma=False,
    )
```

```python
import functools

import jax
import jax.numpy as jnp
from jax import lax
from jax.experimental import pallas as pl
from jax.experimental.pallas import tpu as pltpu
from jax.sharding import PartitionSpec as P

F32 = jnp.float32
BF16 = jnp.bfloat16
LANES = 128
CAPACITY = 4
Z_STRIDE = 16


def mm(a, b):
    return jnp.dot(a, b, preferred_element_type=F32)


def mm_nt(a, b):
    return lax.dot_general(a, b, (((1,), (1,)), ((), ())), preferred_element_type=F32)


def mm_tn(a, b):
    return lax.dot_general(a, b, (((0,), (0,)), ((), ())), preferred_element_type=F32)


def hot(mask):
    return jnp.where(mask, 1.0, 0.0).astype(BF16)


def hot_by_column(row, rows):
    shape = (rows, row.shape[1])
    return hot(lax.broadcasted_iota(jnp.int32, shape, 0) == row)


def hot_by_row(row, columns):
    count = row.shape[1]
    column = jnp.broadcast_to(row, (LANES, count)).T
    lane = lax.broadcasted_iota(jnp.int32, (count, LANES), 1)
    parts = [hot(column == lane + start) for start in range(0, columns, LANES)]
    return jnp.concatenate(parts, axis=1)[:, 0:columns]


def fetch(sems, *pairs):
    copies = [pltpu.make_async_copy(src, dst, sems.at[i]) for i, (src, dst) in enumerate(pairs)]
    for copy in copies:
        copy.start()
    return copies


def join(ref, start, size):
    return jnp.concatenate([ref[q, start : start + size, :] for q in range(ref.shape[0])], axis=1)


def split_high_low(x):
    high = x.astype(BF16)
    return high, (x - high.astype(F32)).astype(BF16)


def pick_sum(hots, x):
    lanes = x.shape[1]
    both = mm(hots, jnp.concatenate(split_high_low(x), axis=1))
    return both[:, 0:lanes] + both[:, lanes:]


def high_low(product, a, x):
    high, low = split_high_low(x)
    return product(a, high) + product(a, low)


def first_kernel(node, rows, picked, node_here, rows_here, picked_here, sems, out_sems):
    copies = fetch(sems, (rows, rows_here), (node, node_here))
    copies[0].wait()
    picks = hot_by_row(rows_here[...], node.shape[0])
    copies[1].wait()
    size = picked.shape[0] // 2
    parts = []
    for i in range(2):
        part = pl.ds(i * size, size)
        picked_here[part, :] = mm(picks[i * size : (i + 1) * size], node_here[...]).astype(BF16)
        parts.append(
            pltpu.make_async_copy(picked_here.at[part, :], picked.at[part, :], out_sems.at[i])
        )
        parts[-1].start()
    for part in parts:
        part.wait()


def early_kernel(region, node, agg, receivers, slots, send_rows, own, indices):
    count = node.shape[0]
    own[0:count, :] = node[...]
    own[count:, :] = agg[...]
    slot = slots[...]
    first = region[0] * CAPACITY
    lane = lax.broadcasted_iota(jnp.int32, send_rows.shape, 1)
    own_row = jnp.full(slot.shape, -1, jnp.int32)
    for k in range(CAPACITY):
        row = jnp.sum(jnp.where(lane == first + k, send_rows[...], 0), axis=1, keepdims=True)
        own_row = jnp.where(slot == first + k, row, own_row)
    other = jnp.where(slot >= first + CAPACITY, slot - CAPACITY, slot)
    other = jnp.where(own_row >= 0, -1, other)
    for i, values in enumerate((receivers[...], slot, other, own_row, send_rows[...])):
        indices[i : i + 1, :] = values


def pack_kernel(region, slot_rows, own, packed):
    start = own.shape[0]
    rest = packed.shape[0] - start
    rows = slot_rows[...].astype(F32)
    place = lax.broadcasted_iota(jnp.int32, (rest, rows.shape[1]), 0)
    kept = jnp.where(place < region[0] * CAPACITY, rows[0:rest, :], rows[CAPACITY:, :])
    packed[0:start, :] = own[...]
    packed[start:, :] = kept.astype(BF16)


def hidden_kernel(
    shared, edge_feat, w_send, w_recv, w_edge, w_out, indices,
    activation, spread, hidden, sems, hidden_sems,
):
    edges, quarter = activation.shape
    feats = spread.shape[0]
    weights = (w_send, w_recv, w_edge)
    blocks = fetch(
        sems,
        *(
            (
                weight.at[q * quarter : (q + 1) * quarter, :],
                spread.at[q, edges + i * quarter : edges + (i + 1) * quarter, :],
            )
            for q in range(feats)
            for i, weight in enumerate(weights)
        ),
    )
    slot_count = edges - CAPACITY
    count = (shared.shape[1] - slot_count) // 2
    at_node = mm(join(shared, 0, count), jnp.concatenate([w_recv[...], w_send[...]], axis=1))
    at_agg = mm(join(shared, count, count), w_out[...])
    at_slot = mm(join(shared, 2 * count, slot_count), w_send[...])
    receive = hot_by_row(indices[0:1, :], count)
    at_edge = pick_sum(receive, jnp.concatenate([at_node[:, 0:quarter], at_agg], axis=1))
    act_grad = at_edge[:, quarter:]
    pre_act = (
        pick_sum(hot_by_row(indices[2:3, :], slot_count), at_slot)
        + pick_sum(hot_by_row(indices[3:4, :], count), at_node[:, quarter:])
        + at_edge[:, 0:quarter]
        + mm(edge_feat[...], w_edge[...])
    )
    gate = jax.nn.sigmoid(pre_act)
    activation[...] = (pre_act * gate).astype(BF16)
    hidden[...] = (act_grad * gate * (1.0 + pre_act * (1.0 - gate))).astype(BF16)
    rows = fetch(
        hidden_sems, *((hidden, spread.at[q, 0:edges, :]) for q in range(feats))
    )
    for copy in (*rows, *blocks):
        copy.wait()


def sender_grads(shared, indices, hidden, out):
    edges = hidden.shape[0]
    slot_count = edges - CAPACITY
    size = out.shape[0] // 2
    quarter = out.shape[1]
    count = (shared.shape[1] - slot_count) // 2
    grad = hidden[...]
    by_slot = mm(hot_by_column(indices[2:3, :], slot_count), grad)
    by_own = mm(hot_by_column(indices[3:4, :], count), grad)
    by_node = mm(hot_by_column(indices[0:1, :], count), grad)
    node_grads = high_low(
        mm_tn, join(shared, 0, count), jnp.concatenate([by_own, by_node], axis=1)
    )
    out[0:size, :] = (
        high_low(mm_tn, join(shared, 2 * count, slot_count), by_slot) + node_grads[:, 0:quarter]
    )
    out[size:, :] = node_grads[:, quarter:]


def edge_grads(shared, indices, hidden, edge_feat, activation, out):
    edges = hidden.shape[0]
    size = out.shape[0] // 2
    count = (shared.shape[1] - edges + CAPACITY) // 2
    out[0:size, :] = mm_tn(edge_feat[...], hidden[...])
    by_agg = mm(hot_by_column(indices[0:1, :], count), activation[...])
    out[size:, :] = high_low(mm_tn, join(shared, count, count), by_agg)


def weight_kernel(other, core, shared, edge_feat, indices, activation, hidden, out):
    first = (core[0] + other) % 2 == 0
    pl.when(first)(lambda: sender_grads(shared, indices, hidden, out))
    pl.when(jnp.logical_not(first))(
        lambda: edge_grads(shared, indices, hidden, edge_feat, activation, out)
    )


def pair_kernel(side, kept, taken, mine, given):
    size = mine.shape[0]
    first, second = (
        kept[i * size : (i + 1) * size, :] + taken[i * size : (i + 1) * size, :] for i in range(2)
    )
    even = side[0] == 0
    mine[...] = jnp.where(even, first, second)
    given[...] = jnp.where(even, second, first).astype(BF16)


def slot_kernel(hidden, indices, terms, edge_grad, recv_part):
    spaces, capacity, quarter = terms.shape
    edges = indices.shape[1]
    full = join(hidden, 0, edges)
    edge_grad[...] = mm_nt(full, join(hidden, edges + 2 * quarter, quarter))
    by_edge = mm_nt(full, join(hidden, edges, quarter))
    sums = pick_sum(hot_by_column(indices[1:2, :], spaces * capacity), by_edge)
    terms[...] = sums.astype(BF16).reshape(terms.shape)
    by_edge = mm_nt(full, join(hidden, edges + quarter, quarter))
    recv_part[...] = pick_sum(hot_by_column(indices[0:1, :], recv_part.shape[0]), by_edge)


def payload_kernel(mine, taken, terms, payload):
    quarter = mine.shape[1]
    total = (mine[...] + taken[...].astype(F32)).astype(BF16)
    payload[:, :, 0:quarter] = total.reshape(terms.shape)
    payload[:, :, quarter:] = terms[...]


def last_kernel(
    arrived, indices, recv_part, edge_here,
    edge_grad, node_grad, grad_send, grad_recv, grad_edge, grad_out, node_here, grads_here, sems,
):
    count, quarter = node_grad.shape
    copies = fetch(sems.at[5:6], (edge_here, edge_grad))
    back = mm(hot_by_column(indices[4:5, :], count), arrived[:, quarter:])
    node_here[...] = recv_part[...] + back
    copies += fetch(sems.at[4:5], (node_here, node_grad))
    shape = (16, arrived.shape[0])
    place = lax.broadcasted_iota(jnp.int32, shape, 1)
    source = place // CAPACITY
    core = source % 2
    side = jnp.where(core == 0, source // 2, source // Z_STRIDE) % 2
    row = (2 * core + side) * CAPACITY + place % CAPACITY
    sums = mm(hot(row == lax.broadcasted_iota(jnp.int32, shape, 0)), arrived[:, 0:quarter])
    outs = (grad_send, grad_recv, grad_edge, grad_out)
    for i, out in enumerate(outs):
        grads_here[i] = sums[i * CAPACITY : (i + 1) * CAPACITY, :]
        copies += fetch(sems.at[i : i + 1], (grads_here.at[i], out))
    for copy in copies:
        copy.wait()


ANY = pl.BlockSpec(memory_space=pl.ANY)
VMEM = pl.BlockSpec(memory_space=pltpu.VMEM)
SMEM = pl.BlockSpec(memory_space=pltpu.SMEM)


def call(kernel, outs, *operands, places=None, out_places=None, scratch=(), flops=0, limit=24 * 1024 * 1024):
    moved = sum(x.size * x.dtype.itemsize for x in operands)
    moved += sum(x.size * x.dtype.itemsize for x in outs)
    return pl.pallas_call(
        kernel,
        out_shape=list(outs),
        in_specs=list(places or [VMEM] * len(operands)),
        out_specs=list(out_places or [VMEM] * len(outs)),
        scratch_shapes=list(scratch),
        compiler_params=pltpu.CompilerParams(vmem_limit_bytes=limit),
        cost_estimate=pl.CostEstimate(flops=flops, bytes_accessed=moved, transcendentals=0),
    )(*operands)


def local(
    node, edge_feat, agg_grad, w_send, w_recv, w_edge, w_out, receivers, edge_slot, send_rows
):
    spaces = lax.axis_size("space")
    feats = lax.axis_size("feat")
    slot_count = send_rows.shape[1]
    capacity = slot_count // spaces
    node_count, quarter = node.shape
    edges, width = edge_feat.shape
    sds = jax.ShapeDtypeStruct
    receivers = receivers.reshape(1, edges)
    slots = edge_slot.reshape(1, edges)
    region = lax.axis_index("space").reshape(1)
    core = region % 2

    def over_feat(x):
        return lax.all_to_all(x, "feat", split_axis=0, concat_axis=0, tiled=True)

    def over_space(x):
        moved = lax.all_to_all(x, "space", split_axis=0, concat_axis=0, tiled=True)
        return moved.reshape(slot_count, x.shape[2])

    (picked,) = call(
        first_kernel,
        (sds((slot_count, quarter), BF16),),
        node, send_rows,
        places=[ANY] * 2,
        scratch=[
            pltpu.VMEM(node.shape, BF16),
            pltpu.VMEM(send_rows.shape, jnp.int32),
            pltpu.VMEM((slot_count, quarter), BF16),
            pltpu.SemaphoreType.DMA((2,)),
            pltpu.SemaphoreType.DMA((2,)),
        ],
        out_places=[ANY],
        flops=2 * slot_count * node_count * quarter,
        limit=60 * 1024 * 1024,
    )
    own, indices = call(
        early_kernel,
        (sds((2 * node_count, quarter), BF16), sds((8, edges), jnp.int32)),
        region, node, agg_grad, receivers, slots, send_rows,
        places=[SMEM] + [VMEM] * 5,
    )
    (packed,) = call(
        pack_kernel,
        (sds((2 * node_count + slot_count - capacity, quarter), BF16),),
        region, over_space(picked.reshape(spaces, capacity, quarter)), own,
        places=[SMEM] + [VMEM] * 2,
    )
    shared = lax.all_gather(packed, "feat", axis=0, tiled=False)
    activation, spread, own_hidden = call(
        hidden_kernel,
        (
            sds((edges, quarter), BF16),
            sds((feats, edges + 3 * quarter, quarter), BF16),
            sds((edges, quarter), BF16),
        ),
        shared, edge_feat, w_send, w_recv, w_edge, w_out, indices,
        out_places=[VMEM, ANY, VMEM],
        scratch=[pltpu.SemaphoreType.DMA((3 * feats,)), pltpu.SemaphoreType.DMA((feats,))],
        flops=2 * edges * width * (2 * node_count + slot_count + 4 * quarter),
    )
    hidden = over_feat(spread)
    given, kept = (
        call(
            functools.partial(weight_kernel, other),
            (sds((2 * width, quarter), F32),),
            core, shared, edge_feat, indices, activation, own_hidden,
            places=[SMEM] + [VMEM] * 5,
            flops=4 * edges * width * quarter,
        )[0]
        for other in (1, 0)
    )
    taken = lax.ppermute(given, "space", [(i, i ^ 1) for i in range(spaces)])
    side = jnp.where(core == 0, region // 2, region // Z_STRIDE) % 2
    mine, given = call(
        pair_kernel,
        (sds((width, quarter), F32), sds((width, quarter), BF16)),
        side, kept, taken,
        places=[SMEM] + [VMEM] * 2,
    )
    taken = lax.ppermute(
        given, "space", [(i, i ^ (Z_STRIDE if i % 2 else 2)) for i in range(spaces)]
    )
    terms, edge_part, recv_part = call(
        slot_kernel,
        (
            sds((spaces, capacity, quarter), BF16),
            sds((edges, quarter), F32),
            sds((node_count, quarter), F32),
        ),
        hidden, indices,
        flops=2 * edges * quarter * (3 * width + 2 * slot_count + 2 * node_count),
    )
    (payload,) = call(
        payload_kernel, (sds((spaces, capacity, 2 * quarter), BF16),), mine, taken, terms
    )
    returned = over_space(payload)
    small = sds((width // spaces, quarter), F32)
    edge_grad, node_grad, grad_send, grad_recv, grad_edge, grad_out = call(
        last_kernel,
        (
            sds((edges, quarter), F32),
            sds((node_count, quarter), F32),
            small, small, small, small,
        ),
        returned, indices, recv_part, edge_part,
        out_places=[ANY] * 6,
        scratch=[
            pltpu.VMEM((node_count, quarter), F32),
            pltpu.VMEM((4, *small.shape), F32),
            pltpu.SemaphoreType.DMA((6,)),
        ],
        flops=2 * slot_count * quarter * (node_count + 16),
    )
    return (node_grad, edge_grad, grad_send, grad_recv, grad_edge, grad_out)


def solution(mesh):
    placed = (
        P("space", "feat"),
        P("space", None),
        P("space", "feat"),
        P(None, "feat"),
        P(None, "feat"),
        P(None, "feat"),
        P(None, "feat"),
        P("space"),
        P("space"),
        P("space", None),
    )
    return jax.shard_map(
        local,
        mesh=mesh,
        in_specs=placed,
        out_specs=(P("space", "feat"),) * 6,
        check_vma=False,
    )
```

```python
import functools

import jax
import jax.numpy as jnp
from jax import lax
from jax.experimental import pallas as pl
from jax.experimental.pallas import tpu as pltpu
from jax.sharding import PartitionSpec as P

F32 = jnp.float32
BF16 = jnp.bfloat16
LANES = 128
CAPACITY = 4
Z_STRIDE = 16


def mm(a, b):
    return jnp.dot(a, b, preferred_element_type=F32)


def mm_nt(a, b):
    return lax.dot_general(a, b, (((1,), (1,)), ((), ())), preferred_element_type=F32)


def mm_tn(a, b):
    return lax.dot_general(a, b, (((0,), (0,)), ((), ())), preferred_element_type=F32)


def hot(mask):
    return jnp.where(mask, 1.0, 0.0).astype(BF16)


def hot_by_column(row, rows):
    shape = (rows, row.shape[1])
    return hot(lax.broadcasted_iota(jnp.int32, shape, 0) == row)


def hot_by_row(row, columns):
    count = row.shape[1]
    column = jnp.broadcast_to(row, (LANES, count)).T
    lane = lax.broadcasted_iota(jnp.int32, (count, LANES), 1)
    parts = [hot(column == lane + start) for start in range(0, columns, LANES)]
    return jnp.concatenate(parts, axis=1)[:, 0:columns]


def fetch(sems, *pairs):
    copies = [pltpu.make_async_copy(src, dst, sems.at[i]) for i, (src, dst) in enumerate(pairs)]
    for copy in copies:
        copy.start()
    return copies


def join(ref, start, size):
    return jnp.concatenate([ref[q, start : start + size, :] for q in range(ref.shape[0])], axis=1)


def split_high_low(x):
    high = x.astype(BF16)
    return high, (x - high.astype(F32)).astype(BF16)


def pick_sum(hots, x):
    lanes = x.shape[1]
    both = mm(hots, jnp.concatenate(split_high_low(x), axis=1))
    return both[:, 0:lanes] + both[:, lanes:]


def high_low(product, a, x):
    high, low = split_high_low(x)
    return product(a, high) + product(a, low)


def first_kernel(node, rows, picked, node_here, rows_here, picked_here, sems, out_sems):
    copies = fetch(sems, (rows, rows_here), (node, node_here))
    copies[0].wait()
    picks = hot_by_row(rows_here[...], node.shape[0])
    copies[1].wait()
    size = picked.shape[0] // 2
    parts = []
    for i in range(2):
        part = pl.ds(i * size, size)
        picked_here[part, :] = mm(picks[i * size : (i + 1) * size], node_here[...]).astype(BF16)
        parts.append(
            pltpu.make_async_copy(picked_here.at[part, :], picked.at[part, :], out_sems.at[i])
        )
        parts[-1].start()
    for part in parts:
        part.wait()


def early_kernel(region, node, agg, receivers, slots, send_rows, own, indices):
    count = node.shape[0]
    own[0:count, :] = node[...]
    own[count:, :] = agg[...]
    slot = slots[...]
    first = region[0] * CAPACITY
    lane = lax.broadcasted_iota(jnp.int32, send_rows.shape, 1)
    own_row = jnp.full(slot.shape, -1, jnp.int32)
    for k in range(CAPACITY):
        row = jnp.sum(jnp.where(lane == first + k, send_rows[...], 0), axis=1, keepdims=True)
        own_row = jnp.where(slot == first + k, row, own_row)
    other = jnp.where(slot >= first + CAPACITY, slot - CAPACITY, slot)
    other = jnp.where(own_row >= 0, -1, other)
    for i, values in enumerate((receivers[...], slot, other, own_row, send_rows[...])):
        indices[i : i + 1, :] = values


def pack_kernel(region, slot_rows, own, packed):
    start = own.shape[0]
    rest = packed.shape[0] - start
    rows = slot_rows[...].astype(F32)
    place = lax.broadcasted_iota(jnp.int32, (rest, rows.shape[1]), 0)
    kept = jnp.where(place < region[0] * CAPACITY, rows[0:rest, :], rows[CAPACITY:, :])
    packed[0:start, :] = own[...]
    packed[start:, :] = kept.astype(BF16)


def hidden_kernel(
    shared, edge_feat, w_send, w_recv, w_edge, w_out, indices,
    activation, spread, hidden, sems, hidden_sems,
):
    edges, quarter = activation.shape
    feats = spread.shape[0]
    weights = (w_send, w_recv, w_edge)
    blocks = fetch(
        sems,
        *(
            (
                weight.at[q * quarter : (q + 1) * quarter, :],
                spread.at[q, edges + i * quarter : edges + (i + 1) * quarter, :],
            )
            for q in range(feats)
            for i, weight in enumerate(weights)
        ),
    )
    slot_count = edges - CAPACITY
    count = (shared.shape[1] - slot_count) // 2
    at_node = mm(join(shared, 0, count), jnp.concatenate([w_recv[...], w_send[...]], axis=1))
    at_agg = mm(join(shared, count, count), w_out[...])
    at_slot = mm(join(shared, 2 * count, slot_count), w_send[...])
    receive = hot_by_row(indices[0:1, :], count)
    at_edge = pick_sum(receive, jnp.concatenate([at_node[:, 0:quarter], at_agg], axis=1))
    act_grad = at_edge[:, quarter:]
    pre_act = (
        pick_sum(hot_by_row(indices[2:3, :], slot_count), at_slot)
        + pick_sum(hot_by_row(indices[3:4, :], count), at_node[:, quarter:])
        + at_edge[:, 0:quarter]
        + mm(edge_feat[...], w_edge[...])
    )
    gate = jax.nn.sigmoid(pre_act)
    activation[...] = (pre_act * gate).astype(BF16)
    hidden[...] = (act_grad * gate * (1.0 + pre_act * (1.0 - gate))).astype(BF16)
    rows = fetch(
        hidden_sems, *((hidden, spread.at[q, 0:edges, :]) for q in range(feats))
    )
    for copy in (*rows, *blocks):
        copy.wait()


def sender_grads(shared, indices, hidden, out):
    edges = hidden.shape[0]
    slot_count = edges - CAPACITY
    size = out.shape[0] // 2
    quarter = out.shape[1]
    count = (shared.shape[1] - slot_count) // 2
    grad = hidden[...]
    by_slot = mm(hot_by_column(indices[2:3, :], slot_count), grad)
    by_own = mm(hot_by_column(indices[3:4, :], count), grad)
    by_node = mm(hot_by_column(indices[0:1, :], count), grad)
    node_grads = high_low(
        mm_tn, join(shared, 0, count), jnp.concatenate([by_own, by_node], axis=1)
    )
    out[0:size, :] = (
        high_low(mm_tn, join(shared, 2 * count, slot_count), by_slot) + node_grads[:, 0:quarter]
    )
    out[size:, :] = node_grads[:, quarter:]


def edge_grads(shared, indices, hidden, edge_feat, activation, out):
    edges = hidden.shape[0]
    size = out.shape[0] // 2
    count = (shared.shape[1] - edges + CAPACITY) // 2
    out[0:size, :] = mm_tn(edge_feat[...], hidden[...])
    by_agg = mm(hot_by_column(indices[0:1, :], count), activation[...])
    out[size:, :] = high_low(mm_tn, join(shared, count, count), by_agg)


def weight_kernel(other, core, shared, edge_feat, indices, activation, hidden, out):
    first = (core[0] + other) % 2 == 0
    pl.when(first)(lambda: sender_grads(shared, indices, hidden, out))
    pl.when(jnp.logical_not(first))(
        lambda: edge_grads(shared, indices, hidden, edge_feat, activation, out)
    )


def pair_kernel(side, kept, taken, mine, given):
    size = mine.shape[0]
    first, second = (
        kept[i * size : (i + 1) * size, :] + taken[i * size : (i + 1) * size, :] for i in range(2)
    )
    even = side[0] == 0
    mine[...] = jnp.where(even, first, second)
    given[...] = jnp.where(even, second, first).astype(BF16)


def slot_kernel(hidden, indices, terms, edge_grad, recv_part):
    spaces, capacity, quarter = terms.shape
    edges = indices.shape[1]
    full = join(hidden, 0, edges)
    edge_grad[...] = mm_nt(full, join(hidden, edges + 2 * quarter, quarter))
    by_edge = mm_nt(full, join(hidden, edges, quarter))
    sums = pick_sum(hot_by_column(indices[1:2, :], spaces * capacity), by_edge)
    terms[...] = sums.astype(BF16).reshape(terms.shape)
    by_edge = mm_nt(full, join(hidden, edges + quarter, quarter))
    recv_part[...] = pick_sum(hot_by_column(indices[0:1, :], recv_part.shape[0]), by_edge)


def payload_kernel(mine, taken, terms, payload):
    quarter = mine.shape[1]
    total = (mine[...] + taken[...].astype(F32)).astype(BF16)
    payload[:, :, 0:quarter] = total.reshape(terms.shape)
    payload[:, :, quarter:] = terms[...]


def last_kernel(
    arrived, indices, recv_part, edge_here,
    edge_grad, node_grad, grad_send, grad_recv, grad_edge, grad_out, node_here, grads_here, sems,
):
    count, quarter = node_grad.shape
    copies = fetch(sems.at[5:6], (edge_here, edge_grad))
    back = mm(hot_by_column(indices[4:5, :], count), arrived[:, quarter:])
    node_here[...] = recv_part[...] + back
    copies += fetch(sems.at[4:5], (node_here, node_grad))
    shape = (16, arrived.shape[0])
    place = lax.broadcasted_iota(jnp.int32, shape, 1)
    source = place // CAPACITY
    core = source % 2
    side = jnp.where(core == 0, source // Z_STRIDE, source // 2) % 2
    row = (2 * core + side) * CAPACITY + place % CAPACITY
    sums = mm(hot(row == lax.broadcasted_iota(jnp.int32, shape, 0)), arrived[:, 0:quarter])
    outs = (grad_send, grad_recv, grad_edge, grad_out)
    for i, out in enumerate(outs):
        grads_here[i] = sums[i * CAPACITY : (i + 1) * CAPACITY, :]
        copies += fetch(sems.at[i : i + 1], (grads_here.at[i], out))
    for copy in copies:
        copy.wait()


ANY = pl.BlockSpec(memory_space=pl.ANY)
VMEM = pl.BlockSpec(memory_space=pltpu.VMEM)
SMEM = pl.BlockSpec(memory_space=pltpu.SMEM)


def call(kernel, outs, *operands, places=None, out_places=None, scratch=(), flops=0, limit=24 * 1024 * 1024):
    moved = sum(x.size * x.dtype.itemsize for x in operands)
    moved += sum(x.size * x.dtype.itemsize for x in outs)
    return pl.pallas_call(
        kernel,
        out_shape=list(outs),
        in_specs=list(places or [VMEM] * len(operands)),
        out_specs=list(out_places or [VMEM] * len(outs)),
        scratch_shapes=list(scratch),
        compiler_params=pltpu.CompilerParams(vmem_limit_bytes=limit),
        cost_estimate=pl.CostEstimate(flops=flops, bytes_accessed=moved, transcendentals=0),
    )(*operands)


def local(
    node, edge_feat, agg_grad, w_send, w_recv, w_edge, w_out, receivers, edge_slot, send_rows
):
    spaces = lax.axis_size("space")
    feats = lax.axis_size("feat")
    slot_count = send_rows.shape[1]
    capacity = slot_count // spaces
    node_count, quarter = node.shape
    edges, width = edge_feat.shape
    sds = jax.ShapeDtypeStruct
    receivers = receivers.reshape(1, edges)
    slots = edge_slot.reshape(1, edges)
    region = lax.axis_index("space").reshape(1)
    core = region % 2

    def over_feat(x):
        return lax.all_to_all(x, "feat", split_axis=0, concat_axis=0, tiled=True)

    def over_space(x):
        moved = lax.all_to_all(x, "space", split_axis=0, concat_axis=0, tiled=True)
        return moved.reshape(slot_count, x.shape[2])

    (picked,) = call(
        first_kernel,
        (sds((slot_count, quarter), BF16),),
        node, send_rows,
        places=[ANY] * 2,
        scratch=[
            pltpu.VMEM(node.shape, BF16),
            pltpu.VMEM(send_rows.shape, jnp.int32),
            pltpu.VMEM((slot_count, quarter), BF16),
            pltpu.SemaphoreType.DMA((2,)),
            pltpu.SemaphoreType.DMA((2,)),
        ],
        out_places=[ANY],
        flops=2 * slot_count * node_count * quarter,
        limit=60 * 1024 * 1024,
    )
    own, indices = call(
        early_kernel,
        (sds((2 * node_count, quarter), BF16), sds((8, edges), jnp.int32)),
        region, node, agg_grad, receivers, slots, send_rows,
        places=[SMEM] + [VMEM] * 5,
    )
    (packed,) = call(
        pack_kernel,
        (sds((2 * node_count + slot_count - capacity, quarter), BF16),),
        region, over_space(picked.reshape(spaces, capacity, quarter)), own,
        places=[SMEM] + [VMEM] * 2,
    )
    shared = lax.all_gather(packed, "feat", axis=0, tiled=False)
    activation, spread, own_hidden = call(
        hidden_kernel,
        (
            sds((edges, quarter), BF16),
            sds((feats, edges + 3 * quarter, quarter), BF16),
            sds((edges, quarter), BF16),
        ),
        shared, edge_feat, w_send, w_recv, w_edge, w_out, indices,
        out_places=[VMEM, ANY, VMEM],
        scratch=[pltpu.SemaphoreType.DMA((3 * feats,)), pltpu.SemaphoreType.DMA((feats,))],
        flops=2 * edges * width * (2 * node_count + slot_count + 4 * quarter),
    )
    hidden = over_feat(spread)
    given, kept = (
        call(
            functools.partial(weight_kernel, other),
            (sds((2 * width, quarter), F32),),
            core, shared, edge_feat, indices, activation, own_hidden,
            places=[SMEM] + [VMEM] * 5,
            flops=4 * edges * width * quarter,
        )[0]
        for other in (1, 0)
    )
    taken = lax.ppermute(given, "space", [(i, i ^ 1) for i in range(spaces)])
    side = jnp.where(core == 0, region // Z_STRIDE, region // 2) % 2
    mine, given = call(
        pair_kernel,
        (sds((width, quarter), F32), sds((width, quarter), BF16)),
        side, kept, taken,
        places=[SMEM] + [VMEM] * 2,
    )
    taken = lax.ppermute(
        given, "space", [(i, i ^ (2 if i % 2 else Z_STRIDE)) for i in range(spaces)]
    )
    terms, edge_part, recv_part = call(
        slot_kernel,
        (
            sds((spaces, capacity, quarter), BF16),
            sds((edges, quarter), F32),
            sds((node_count, quarter), F32),
        ),
        hidden, indices,
        flops=2 * edges * quarter * (3 * width + 2 * slot_count + 2 * node_count),
    )
    (payload,) = call(
        payload_kernel, (sds((spaces, capacity, 2 * quarter), BF16),), mine, taken, terms
    )
    returned = over_space(payload)
    small = sds((width // spaces, quarter), F32)
    edge_grad, node_grad, grad_send, grad_recv, grad_edge, grad_out = call(
        last_kernel,
        (
            sds((edges, quarter), F32),
            sds((node_count, quarter), F32),
            small, small, small, small,
        ),
        returned, indices, recv_part, edge_part,
        out_places=[ANY] * 6,
        scratch=[
            pltpu.VMEM((node_count, quarter), F32),
            pltpu.VMEM((4, *small.shape), F32),
            pltpu.SemaphoreType.DMA((6,)),
        ],
        flops=2 * slot_count * quarter * (node_count + 16),
    )
    return (node_grad, edge_grad, grad_send, grad_recv, grad_edge, grad_out)


def solution(mesh):
    placed = (
        P("space", "feat"),
        P("space", None),
        P("space", "feat"),
        P(None, "feat"),
        P(None, "feat"),
        P(None, "feat"),
        P(None, "feat"),
        P("space"),
        P("space"),
        P("space", None),
    )
    return jax.shard_map(
        local,
        mesh=mesh,
        in_specs=placed,
        out_specs=(P("space", "feat"),) * 6,
        check_vma=False,
    )
```

```python
import functools

import jax
import jax.numpy as jnp
from jax import lax
from jax.experimental import pallas as pl
from jax.experimental.pallas import tpu as pltpu
from jax.sharding import PartitionSpec as P

F32 = jnp.float32
BF16 = jnp.bfloat16
LANES = 128
CAPACITY = 4
Z_STRIDE = 16


def mm(a, b):
    return jnp.dot(a, b, preferred_element_type=F32)


def mm_nt(a, b):
    return lax.dot_general(a, b, (((1,), (1,)), ((), ())), preferred_element_type=F32)


def mm_tn(a, b):
    return lax.dot_general(a, b, (((0,), (0,)), ((), ())), preferred_element_type=F32)


def hot(mask):
    return jnp.where(mask, 1.0, 0.0).astype(BF16)


def hot_by_column(row, rows):
    shape = (rows, row.shape[1])
    return hot(lax.broadcasted_iota(jnp.int32, shape, 0) == row)


def hot_by_row(row, columns):
    count = row.shape[1]
    column = jnp.broadcast_to(row, (LANES, count)).T
    lane = lax.broadcasted_iota(jnp.int32, (count, LANES), 1)
    parts = [hot(column == lane + start) for start in range(0, columns, LANES)]
    return jnp.concatenate(parts, axis=1)[:, 0:columns]


def fetch(sems, *pairs):
    copies = [pltpu.make_async_copy(src, dst, sems.at[i]) for i, (src, dst) in enumerate(pairs)]
    for copy in copies:
        copy.start()
    return copies


def join(ref, start, size):
    return jnp.concatenate([ref[q, start : start + size, :] for q in range(ref.shape[0])], axis=1)


def split_high_low(x):
    high = x.astype(BF16)
    return high, (x - high.astype(F32)).astype(BF16)


def pick_sum(hots, x):
    lanes = x.shape[1]
    both = mm(hots, jnp.concatenate(split_high_low(x), axis=1))
    return both[:, 0:lanes] + both[:, lanes:]


def high_low(product, a, x):
    high, low = split_high_low(x)
    return product(a, high) + product(a, low)


def first_kernel(node, rows, picked, node_here, rows_here, picked_here, sems, out_sems):
    copies = fetch(sems, (rows, rows_here), (node, node_here))
    copies[0].wait()
    picks = hot_by_row(rows_here[...], node.shape[0])
    copies[1].wait()
    size = picked.shape[0] // 2
    parts = []
    for i in range(2):
        part = pl.ds(i * size, size)
        picked_here[part, :] = mm(picks[i * size : (i + 1) * size], node_here[...]).astype(BF16)
        parts.append(
            pltpu.make_async_copy(picked_here.at[part, :], picked.at[part, :], out_sems.at[i])
        )
        parts[-1].start()
    for part in parts:
        part.wait()


def early_kernel(region, node, agg, receivers, slots, send_rows, own, indices):
    count = node.shape[0]
    own[0:count, :] = node[...]
    own[count:, :] = agg[...]
    slot = slots[...]
    first = region[0] * CAPACITY
    lane = lax.broadcasted_iota(jnp.int32, send_rows.shape, 1)
    own_row = jnp.full(slot.shape, -1, jnp.int32)
    for k in range(CAPACITY):
        row = jnp.sum(jnp.where(lane == first + k, send_rows[...], 0), axis=1, keepdims=True)
        own_row = jnp.where(slot == first + k, row, own_row)
    other = jnp.where(slot >= first + CAPACITY, slot - CAPACITY, slot)
    other = jnp.where(own_row >= 0, -1, other)
    for i, values in enumerate((receivers[...], slot, other, own_row, send_rows[...])):
        indices[i : i + 1, :] = values


def pack_kernel(region, slot_rows, own, packed):
    start = own.shape[0]
    rest = packed.shape[0] - start
    rows = slot_rows[...].astype(F32)
    place = lax.broadcasted_iota(jnp.int32, (rest, rows.shape[1]), 0)
    kept = jnp.where(place < region[0] * CAPACITY, rows[0:rest, :], rows[CAPACITY:, :])
    packed[0:start, :] = own[...]
    packed[start:, :] = kept.astype(BF16)


def hidden_kernel(
    shared, edge_feat, w_send, w_recv, w_edge, w_out, indices,
    activation, spread, hidden, sems, hidden_sems,
):
    edges, quarter = activation.shape
    feats = spread.shape[0]
    weights = (w_send, w_recv, w_edge)
    blocks = fetch(
        sems,
        *(
            (
                weight.at[q * quarter : (q + 1) * quarter, :],
                spread.at[q, edges + i * quarter : edges + (i + 1) * quarter, :],
            )
            for q in range(feats)
            for i, weight in enumerate(weights)
        ),
    )
    slot_count = edges - CAPACITY
    count = (shared.shape[1] - slot_count) // 2
    at_node = mm(join(shared, 0, count), jnp.concatenate([w_recv[...], w_send[...]], axis=1))
    at_agg = mm(join(shared, count, count), w_out[...])
    at_slot = mm(join(shared, 2 * count, slot_count), w_send[...])
    receive = hot_by_row(indices[0:1, :], count)
    at_edge = pick_sum(receive, jnp.concatenate([at_node[:, 0:quarter], at_agg], axis=1))
    act_grad = at_edge[:, quarter:]
    pre_act = (
        pick_sum(hot_by_row(indices[2:3, :], slot_count), at_slot)
        + pick_sum(hot_by_row(indices[3:4, :], count), at_node[:, quarter:])
        + at_edge[:, 0:quarter]
        + mm(edge_feat[...], w_edge[...])
    )
    gate = jax.nn.sigmoid(pre_act)
    hidden[...] = (act_grad * gate * (1.0 + pre_act * (1.0 - gate))).astype(BF16)
    rows = fetch(
        hidden_sems, *((hidden, spread.at[q, 0:edges, :]) for q in range(feats))
    )
    activation[...] = (pre_act * gate).astype(BF16)
    for copy in (*rows, *blocks):
        copy.wait()


def sender_grads(shared, indices, hidden, out):
    edges = hidden.shape[0]
    slot_count = edges - CAPACITY
    size = out.shape[0] // 2
    quarter = out.shape[1]
    count = (shared.shape[1] - slot_count) // 2
    grad = hidden[...]
    by_slot = mm(hot_by_column(indices[2:3, :], slot_count), grad)
    by_own = mm(hot_by_column(indices[3:4, :], count), grad)
    by_node = mm(hot_by_column(indices[0:1, :], count), grad)
    node_grads = high_low(
        mm_tn, join(shared, 0, count), jnp.concatenate([by_own, by_node], axis=1)
    )
    out[0:size, :] = (
        high_low(mm_tn, join(shared, 2 * count, slot_count), by_slot) + node_grads[:, 0:quarter]
    )
    out[size:, :] = node_grads[:, quarter:]


def edge_grads(shared, indices, hidden, edge_feat, activation, out):
    edges = hidden.shape[0]
    size = out.shape[0] // 2
    count = (shared.shape[1] - edges + CAPACITY) // 2
    out[0:size, :] = mm_tn(edge_feat[...], hidden[...])
    by_agg = mm(hot_by_column(indices[0:1, :], count), activation[...])
    out[size:, :] = high_low(mm_tn, join(shared, count, count), by_agg)


def weight_kernel(other, core, shared, edge_feat, indices, activation, hidden, out):
    first = (core[0] + other) % 2 == 0
    pl.when(first)(lambda: sender_grads(shared, indices, hidden, out))
    pl.when(jnp.logical_not(first))(
        lambda: edge_grads(shared, indices, hidden, edge_feat, activation, out)
    )


def pair_kernel(side, kept, taken, mine, given):
    size = mine.shape[0]
    first, second = (
        kept[i * size : (i + 1) * size, :] + taken[i * size : (i + 1) * size, :] for i in range(2)
    )
    even = side[0] == 0
    mine[...] = jnp.where(even, first, second)
    given[...] = jnp.where(even, second, first).astype(BF16)


def slot_kernel(hidden, indices, terms, edge_grad, recv_part):
    spaces, capacity, quarter = terms.shape
    edges = indices.shape[1]
    full = join(hidden, 0, edges)
    edge_grad[...] = mm_nt(full, join(hidden, edges + 2 * quarter, quarter))
    by_edge = mm_nt(full, join(hidden, edges, quarter))
    sums = pick_sum(hot_by_column(indices[1:2, :], spaces * capacity), by_edge)
    terms[...] = sums.astype(BF16).reshape(terms.shape)
    by_edge = mm_nt(full, join(hidden, edges + quarter, quarter))
    recv_part[...] = pick_sum(hot_by_column(indices[0:1, :], recv_part.shape[0]), by_edge)


def payload_kernel(mine, taken, terms, payload):
    quarter = mine.shape[1]
    total = (mine[...] + taken[...].astype(F32)).astype(BF16)
    payload[:, :, 0:quarter] = total.reshape(terms.shape)
    payload[:, :, quarter:] = terms[...]


def last_kernel(
    arrived, indices, recv_part, edge_here,
    edge_grad, node_grad, grad_send, grad_recv, grad_edge, grad_out, node_here, grads_here, sems,
):
    count, quarter = node_grad.shape
    copies = fetch(sems.at[5:6], (edge_here, edge_grad))
    back = mm(hot_by_column(indices[4:5, :], count), arrived[:, quarter:])
    node_here[...] = recv_part[...] + back
    copies += fetch(sems.at[4:5], (node_here, node_grad))
    shape = (16, arrived.shape[0])
    place = lax.broadcasted_iota(jnp.int32, shape, 1)
    source = place // CAPACITY
    core = source % 2
    side = jnp.where(core == 0, source // 2, source // Z_STRIDE) % 2
    row = (2 * core + side) * CAPACITY + place % CAPACITY
    sums = mm(hot(row == lax.broadcasted_iota(jnp.int32, shape, 0)), arrived[:, 0:quarter])
    outs = (grad_send, grad_recv, grad_edge, grad_out)
    for i, out in enumerate(outs):
        grads_here[i] = sums[i * CAPACITY : (i + 1) * CAPACITY, :]
        copies += fetch(sems.at[i : i + 1], (grads_here.at[i], out))
    for copy in copies:
        copy.wait()


ANY = pl.BlockSpec(memory_space=pl.ANY)
VMEM = pl.BlockSpec(memory_space=pltpu.VMEM)
SMEM = pl.BlockSpec(memory_space=pltpu.SMEM)


def call(kernel, outs, *operands, places=None, out_places=None, scratch=(), flops=0, limit=24 * 1024 * 1024):
    moved = sum(x.size * x.dtype.itemsize for x in operands)
    moved += sum(x.size * x.dtype.itemsize for x in outs)
    return pl.pallas_call(
        kernel,
        out_shape=list(outs),
        in_specs=list(places or [VMEM] * len(operands)),
        out_specs=list(out_places or [VMEM] * len(outs)),
        scratch_shapes=list(scratch),
        compiler_params=pltpu.CompilerParams(vmem_limit_bytes=limit),
        cost_estimate=pl.CostEstimate(flops=flops, bytes_accessed=moved, transcendentals=0),
    )(*operands)


def local(
    node, edge_feat, agg_grad, w_send, w_recv, w_edge, w_out, receivers, edge_slot, send_rows
):
    spaces = lax.axis_size("space")
    feats = lax.axis_size("feat")
    slot_count = send_rows.shape[1]
    capacity = slot_count // spaces
    node_count, quarter = node.shape
    edges, width = edge_feat.shape
    sds = jax.ShapeDtypeStruct
    receivers = receivers.reshape(1, edges)
    slots = edge_slot.reshape(1, edges)
    region = lax.axis_index("space").reshape(1)
    core = region % 2

    def over_feat(x):
        return lax.all_to_all(x, "feat", split_axis=0, concat_axis=0, tiled=True)

    def over_space(x):
        moved = lax.all_to_all(x, "space", split_axis=0, concat_axis=0, tiled=True)
        return moved.reshape(slot_count, x.shape[2])

    (picked,) = call(
        first_kernel,
        (sds((slot_count, quarter), BF16),),
        node, send_rows,
        places=[ANY] * 2,
        scratch=[
            pltpu.VMEM(node.shape, BF16),
            pltpu.VMEM(send_rows.shape, jnp.int32),
            pltpu.VMEM((slot_count, quarter), BF16),
            pltpu.SemaphoreType.DMA((2,)),
            pltpu.SemaphoreType.DMA((2,)),
        ],
        out_places=[ANY],
        flops=2 * slot_count * node_count * quarter,
        limit=60 * 1024 * 1024,
    )
    own, indices = call(
        early_kernel,
        (sds((2 * node_count, quarter), BF16), sds((8, edges), jnp.int32)),
        region, node, agg_grad, receivers, slots, send_rows,
        places=[SMEM] + [VMEM] * 5,
    )
    (packed,) = call(
        pack_kernel,
        (sds((2 * node_count + slot_count - capacity, quarter), BF16),),
        region, over_space(picked.reshape(spaces, capacity, quarter)), own,
        places=[SMEM] + [VMEM] * 2,
    )
    shared = lax.all_gather(packed, "feat", axis=0, tiled=False)
    activation, spread, own_hidden = call(
        hidden_kernel,
        (
            sds((edges, quarter), BF16),
            sds((feats, edges + 3 * quarter, quarter), BF16),
            sds((edges, quarter), BF16),
        ),
        shared, edge_feat, w_send, w_recv, w_edge, w_out, indices,
        out_places=[VMEM, ANY, VMEM],
        scratch=[pltpu.SemaphoreType.DMA((3 * feats,)), pltpu.SemaphoreType.DMA((feats,))],
        flops=2 * edges * width * (2 * node_count + slot_count + 4 * quarter),
    )
    hidden = over_feat(spread)
    given, kept = (
        call(
            functools.partial(weight_kernel, other),
            (sds((2 * width, quarter), F32),),
            core, shared, edge_feat, indices, activation, own_hidden,
            places=[SMEM] + [VMEM] * 5,
            flops=4 * edges * width * quarter,
        )[0]
        for other in (1, 0)
    )
    taken = lax.ppermute(given, "space", [(i, i ^ 1) for i in range(spaces)])
    side = jnp.where(core == 0, region // 2, region // Z_STRIDE) % 2
    mine, given = call(
        pair_kernel,
        (sds((width, quarter), F32), sds((width, quarter), BF16)),
        side, kept, taken,
        places=[SMEM] + [VMEM] * 2,
    )
    taken = lax.ppermute(
        given, "space", [(i, i ^ (Z_STRIDE if i % 2 else 2)) for i in range(spaces)]
    )
    terms, edge_part, recv_part = call(
        slot_kernel,
        (
            sds((spaces, capacity, quarter), BF16),
            sds((edges, quarter), F32),
            sds((node_count, quarter), F32),
        ),
        hidden, indices,
        flops=2 * edges * quarter * (3 * width + 2 * slot_count + 2 * node_count),
    )
    (payload,) = call(
        payload_kernel, (sds((spaces, capacity, 2 * quarter), BF16),), mine, taken, terms
    )
    returned = over_space(payload)
    small = sds((width // spaces, quarter), F32)
    edge_grad, node_grad, grad_send, grad_recv, grad_edge, grad_out = call(
        last_kernel,
        (
            sds((edges, quarter), F32),
            sds((node_count, quarter), F32),
            small, small, small, small,
        ),
        returned, indices, recv_part, edge_part,
        out_places=[ANY] * 6,
        scratch=[
            pltpu.VMEM((node_count, quarter), F32),
            pltpu.VMEM((4, *small.shape), F32),
            pltpu.SemaphoreType.DMA((6,)),
        ],
        flops=2 * slot_count * quarter * (node_count + 16),
    )
    return (node_grad, edge_grad, grad_send, grad_recv, grad_edge, grad_out)


def solution(mesh):
    placed = (
        P("space", "feat"),
        P("space", None),
        P("space", "feat"),
        P(None, "feat"),
        P(None, "feat"),
        P(None, "feat"),
        P(None, "feat"),
        P("space"),
        P("space"),
        P("space", None),
    )
    return jax.shard_map(
        local,
        mesh=mesh,
        in_specs=placed,
        out_specs=(P("space", "feat"),) * 6,
        check_vma=False,
    )
```
